32 devices in a mesh: groups: 2 (over x), replica: 2 (over core), tensor: 8 (over z, y).
Axes of the slice: x: 2, y: 2, z: 4, core: 2. Of those that a mesh axis runs over, the one named last changes fastest.
Arguments:
- hidden: bfloat16 [128, 8192], P(('groups', 'replica'), 'tensor'), parts along dimension 0, may hold values from -6 to 6
- w_query: bfloat16 [8192, 8192], P(None, 'tensor'), may hold values from -0.0625 to 0.0625
- output_weight: bfloat16 [8192, 8192], P('tensor'), may hold values from -0.09375 to 0.09375
- keys: bfloat16 [128, 8, 32, 128], P(('groups', 'replica')), parts along dimension 0
- values: bfloat16 [128, 8, 32, 128], P(('groups', 'replica')), parts along dimension 0, may hold values from -6 to 6
- query_down_maps: bfloat16 [16, 64, 8192], P(('groups', 'replica'), None, 'tensor'), parts along dimension 0, may hold values from -0.0625 to 0.0625
- query_up_maps: bfloat16 [16, 64, 8192], P(('groups', 'replica'), None, 'tensor'), parts along dimension 0, may hold values from -0.75 to 0.75
- output_down_maps: bfloat16 [16, 64, 8192], P(('groups', 'replica'), None, 'tensor'), parts along dimension 0, may hold values from -0.0625 to 0.0625
- output_up_maps: bfloat16 [16, 64, 8192], P(('groups', 'replica'), None, 'tensor'), parts along dimension 0, may hold values from -0.75 to 0.75
- adapter_ids: int32 [128], P('groups'), parts along dimension 0, may hold values from 0 to 7
- owner_map: int32 [16], P('groups'), parts along dimension 0, may hold values from 0 to 7, each once
- kv_lengths: int32 [128], P(('groups', 'replica')), parts along dimension 0, may hold values from 1 to 32, as said below
Outputs:
- attn_out: bfloat16 [128, 8192], P(('groups', 'replica'), 'tensor'), parts along dimension 0
The draws below stay inside these ranges and needn't reach their ends.
There are 2 independent parts, one for each index of `groups`. The reference program is written for one: setup_inputs(seed, part) draws one part's arguments, and reference() takes and returns one part's arrays. A program takes and returns all parts, laid end to end along the dimension named above; an argument that names none is the same for every part. Nothing has to cross between parts.
Inputs may be any that keep to these rules, and one draw needn't show every extreme that they name: `owner_map`: every request's adapter has a slot; slot s is stored at replica index s // 4. Request r attends to its first kv_lengths[r] cached positions; some request holds all 32.
All inputs are finite; a program needn't handle non-finite values.
Results may differ from the reference program's by a relative error of at most 0.0092.
Values may be sent and summed in bfloat16 or wider, within the bound.
A program may use at most 128 MiB of HBM per device.

```python
import math
import jax
import jax.numpy as jnp
import numpy as np
from jax import lax

D = 8192
HEADS = 64
HD = 128
KVS = 8
RANK = 64
LEN = 32
QW = 8192
REQS = 64
ADAPTERS = 8


def draw_keys(key, part):
    first = jax.random.fold_in(key, 11)
    drawn_projection = jax.random.normal(first, (REQS, KVS, LEN, HD), jnp.float32)
    return drawn_projection.astype(jnp.bfloat16)


def draw_kv_lengths(key, part):
    lengths = jax.random.randint(jax.random.fold_in(key, 21), (REQS,), 1, LEN + 1, dtype=jnp.int32)
    return lengths.at[0].set(LEN)


def place_ends(array, rng, least, largest):
    shape = array.shape
    spot = [jax.random.randint(jax.random.fold_in(rng, axis), (), 0, shape[axis]) for axis in range(len(shape))]
    array = array.at[tuple(spot)].set(least)
    longest = shape.index(max(shape))
    spot[longest] = (spot[longest] + 1) % shape[longest]
    return array.at[tuple(spot)].set(largest)


def strengthened(array, stream_key, source, target, shards_of, factor):
    def block_of(dim):
        return (jnp.arange(array.shape[dim]) // (array.shape[dim] // shards_of)).reshape((-1,) + (1,) * (array.ndim - 1 - dim))

    near = jax.random.permutation(stream_key, shards_of)[block_of(target)]
    second = (block_of(target) + shards_of // 2) % shards_of
    return jnp.where((block_of(source) == near) | (block_of(source) == second), factor * array, array)


def block_levels(own_key, shape, shards, smallest, high):
    loudness = 1.0
    for dim, parts in shards:
        draws = jax.random.uniform(jax.random.fold_in(jax.random.fold_in(own_key, 6), dim), (parts,), jnp.float32, smallest / len(shards), high / len(shards))
        loudness = loudness * jnp.repeat(jnp.exp(draws), shape[dim] // parts).reshape((-1,) + (1,) * (len(shape) - 1 - dim))
    return loudness


def rank_bounds(number_of, skew):
    portions = [(1 << 20) // math.isqrt(standing ** skew) + 1 for standing in range(1, number_of + 1)]
    spread = 1 + sum(portions) // (1 << 30)
    return np.cumsum(np.array([max(1, weight // spread) for weight in portions]))


def skewed_ids(stream_key, shape, count, slope):
    table = rank_bounds(count, slope)
    ticket = jax.random.randint(jax.random.fold_in(stream_key, 1), shape, 0, int(table[count - 1]))
    standing = jnp.searchsorted(jnp.asarray(table, jnp.int32), ticket, side="right")
    return jax.random.permutation(jax.random.fold_in(stream_key, 2), count)[standing].astype(jnp.int32)


def noise(stream_key, dims, spread, bound, split=(), kind=jnp.bfloat16):
    loudness = block_levels(stream_key, dims, split, -0.22, 0.18) if split else 1.0
    drawn = jax.random.normal(stream_key, dims, jnp.float32) * spread * loudness
    return jnp.minimum(jnp.maximum(drawn, -bound), bound).astype(kind)


def bell_draw_with(key, shape, deviation, most, shards, heavy, kind=jnp.bfloat16):
    result = deviation * jax.random.normal(key, shape, jnp.float32)
    if shards:
        result = result * block_levels(key, shape, shards, -0.22, 0.18)
    return jnp.clip(strengthened(result, jax.random.fold_in(key, 3), *heavy), -most, most).astype(kind)


def setup_inputs(seed: int = 0, part: int = 0) -> dict:
    streams_of = jax.random.split(jax.random.key(seed), 13)
    part_keys = jax.random.split(jax.random.fold_in(streams_of[12], part), 13)
    return {
        "hidden": noise(part_keys[0], (REQS, D), 1.0, 6.0, ((0, 2), (1, 8))),
        "w_query": noise(streams_of[1], (D, QW), D ** -0.5, 0.0625, ((1, 8),)),
        "output_weight": bell_draw_with(streams_of[2], (QW, D), QW ** -0.5, 0.09375, ((0, 8),), (0, 1, 8, 2.0)),
        "keys": draw_keys(jax.random.fold_in(jax.random.fold_in(streams_of[12], part), 71), part),
        "values": noise(part_keys[4], (REQS, KVS, LEN, HD), 1.0, 6.0, ((0, 2),)),
        "query_down_maps": noise(part_keys[5], (ADAPTERS, RANK, D), D ** -0.5, 0.0625, ((0, 2), (2, 8))),
        "query_up_maps": noise(part_keys[6], (ADAPTERS, RANK, QW), RANK ** -0.5, 0.75, ((0, 2), (2, 8))),
        "output_down_maps": noise(part_keys[7], (ADAPTERS, RANK, QW), QW ** -0.5, 0.0625, ((0, 2), (2, 8))),
        "output_up_maps": noise(part_keys[8], (ADAPTERS, RANK, D), RANK ** -0.5, 0.75, ((0, 2), (2, 8))),
        "adapter_ids": place_ends(skewed_ids(part_keys[9], (REQS,), ADAPTERS, 2), jax.random.fold_in(part_keys[9], 3), 0, ADAPTERS - 1).astype(jnp.int32),
        "owner_map": jax.random.permutation(part_keys[10], ADAPTERS).astype(jnp.int32),
        "kv_lengths": draw_kv_lengths(jax.random.fold_in(jax.random.fold_in(streams_of[12], part), 71), part),
    }


def reference(hidden, w_query, output_weight, keys, values, query_down_maps, query_up_maps, output_down_maps, output_up_maps, adapter_ids, owner_map, kv_lengths):
    slot = owner_map[adapter_ids].astype(jnp.int32)
    pick = (slot[:, None] == jnp.arange(ADAPTERS, dtype=jnp.int32)[None, :]).astype(jnp.float32)

    def adapter_delta(input_rows, down_product, up_product):
        part = jnp.einsum('ah,fth->aft', input_rows.astype(jnp.float32), down_product.astype(jnp.float32))
        low = lax.optimization_barrier(jnp.sum(pick[:, :, None] * part, axis=1)).astype(jnp.bfloat16)
        spread_rows = pick[:, :, None] * low.astype(jnp.float32)[:, None, :]
        return jnp.einsum('xpl,ply->xy', spread_rows, up_product.astype(jnp.float32))
    plain_projection = jnp.dot(hidden, w_query, preferred_element_type=jnp.float32)
    query_rows = (plain_projection + 0.5 * adapter_delta(hidden, query_down_maps, query_up_maps)).astype(jnp.bfloat16)
    heads_q = query_rows.astype(jnp.float32).reshape(REQS, KVS, HEADS // KVS, HD)
    scores = jnp.einsum('rkhd,rkld->rkhl', heads_q, keys.astype(jnp.float32)) / math.sqrt(HD)
    live = jnp.arange(LEN, dtype=jnp.int32)[None, None, None, :] < kv_lengths[:, None, None, None]
    scores = jnp.where(live, scores, -1e+30)
    top = lax.optimization_barrier(jnp.max(scores, axis=-1, keepdims=True))
    weights = jnp.exp(scores - top)
    probs = (weights / lax.optimization_barrier(jnp.sum(weights, axis=-1, keepdims=True))).astype(jnp.bfloat16)
    combined_output = jnp.einsum('rkhl,rkld->rkhd', probs.astype(jnp.float32), values.astype(jnp.float32))
    combined_output = combined_output.astype(jnp.bfloat16).reshape(REQS, QW)
    final_output = jnp.dot(combined_output, output_weight, preferred_element_type=jnp.float32) + 0.5 * adapter_delta(combined_output, output_down_maps, output_up_maps)
    return final_output.astype(jnp.bfloat16)
```

```python
import functools
import math

import jax
import jax.numpy as jnp
from jax import lax
from jax.experimental import pallas as pl
from jax.experimental.pallas import tpu as pltpu
from jax.sharding import PartitionSpec as P

HEADS = 64
KVS = 8
ROW_BLOCK = 8
F32 = jnp.float32
BF16 = jnp.bfloat16


def loop(count, body, first=0):
    def step(k, carry):
        body(k)
        return carry

    if count > first:
        lax.fori_loop(first, count, step, 0)


def remote(src, dst, send_sem, recv_sem, device):
    return pltpu.make_async_remote_copy(
        src_ref=src,
        dst_ref=dst,
        send_sem=send_sem,
        recv_sem=recv_sem,
        device_id=device,
        device_id_type=pl.DeviceIdType.MESH,
    )


def block_kernel(
    tensor,
    replicas,
    hidden,
    w_query,
    output_weight,
    keys,
    values,
    query_down,
    query_up,
    output_down,
    output_up,
    slots,
    lengths,
    out,
    h_buf,
    wq_buf,
    ow_buf,
    key_buf,
    value_buf,
    map_buf,
    acc,
    mixed,
    low_send,
    low_recv,
    pair_send,
    pair_recv,
    far_send,
    far_recv,
    h_local,
    wq_sem,
    ow_sem,
    kv_sem,
    map_local,
    map_send_sem,
    map_recv_sem,
    h_send_sem,
    h_recv_sem,
    fwd_send_sem,
    low_send_sem,
    low_recv_sem,
    pair_send_sem,
    pair_recv_sem,
    far_send_sem,
    far_recv_sem,
):
    rows, width = hidden.shape
    cols = w_query.shape[1]
    head_size = keys.shape[3]
    length = keys.shape[2]
    stored, rank, _ = query_down.shape
    adapters = stored * replicas
    lanes = low_send.shape[2]
    inner = 2 if tensor % 2 == 0 else 1
    outer = tensor // inner
    me = lax.axis_index("tensor")
    rep = lax.axis_index("replica")
    o, i = me // inner, me % inner

    def at(k, j):
        return ((o + k) % outer) * inner + (i + j) % inner

    barrier = pltpu.get_barrier_semaphore()
    for k in range(1, tensor):
        pl.semaphore_signal(
            barrier, inc=1, device_id={"tensor": (me + k) % tensor}, device_id_type=pl.DeviceIdType.MESH
        )
    for k in range(1, replicas):
        pl.semaphore_signal(
            barrier, inc=1, device_id={"replica": (rep + k) % replicas}, device_id_type=pl.DeviceIdType.MESH
        )

    own_hidden = pltpu.make_async_copy(hidden, h_buf.at[me], h_local)
    own_hidden.start()
    maps = (query_down, query_up, output_down, output_up)
    own_slots = pl.ds(pl.multiple_of(rep * stored, stored), stored)
    own_maps = [
        pltpu.make_async_copy(maps[m], map_buf.at[m, own_slots], map_local.at[m]) for m in range(4)
    ]
    order = [(k, j) for j in range(inner) for k in range(outer)]

    def wq_copy(s):
        return pltpu.make_async_copy(
            w_query.at[pl.ds(pl.multiple_of(s * width, width), width), :], wq_buf.at[s], wq_sem.at[s]
        )

    def ow_copy(s):
        return pltpu.make_async_copy(
            output_weight.at[:, pl.ds(pl.multiple_of(s * width, width), width)], ow_buf.at[s], ow_sem.at[s]
        )

    own_maps[0].start()
    local_heads = cols // head_size
    group = HEADS // KVS
    kv_count = max(1, local_heads // group)
    first_kv = me * local_heads // group
    kv_copies = []
    for j in range(kv_count):
        kv_copies.append(pltpu.make_async_copy(keys.at[:, first_kv + j], key_buf.at[j], kv_sem.at[0, j]))
        kv_copies.append(pltpu.make_async_copy(values.at[:, first_kv + j], value_buf.at[j], kv_sem.at[1, j]))
    for k, j in order:
        wq_copy(at(k, j)).start()

    pl.semaphore_wait(barrier, tensor - 1 + replicas - 1)
    own_hidden.wait()

    h_sends = []
    for k in range(1, outer):
        h_sends.append(
            remote(
                h_buf.at[me], h_buf.at[me], h_send_sem.at[k], h_recv_sem.at[me], {"tensor": at(k, 0)}
            )
        )
    if inner == 2:
        h_sends.append(
            remote(h_buf.at[me], h_buf.at[me], h_send_sem.at[0], h_recv_sem.at[me], {"tensor": at(0, 1)})
        )
    for copy in h_sends:
        copy.start()

    map_copies = []
    for m in range(4):
        for k in range(1, replicas):
            map_copies.append(
                remote(
                    maps[m],
                    map_buf.at[m, own_slots],
                    map_send_sem.at[m, k],
                    map_recv_sem.at[m, rep],
                    {"replica": (rep + k) % replicas},
                )
            )
            map_copies[-1].start()
    for m in range(1, 4):
        own_maps[m].start()
    for copy in kv_copies:
        copy.start()
    for k, j in [(k, j) for j in reversed(range(inner)) for k in list(range(1, outer)) + [0]]:
        ow_copy(at(k, j)).start()

    def wait_map(m):
        own_maps[m].wait()
        for k in range(1, replicas):
            other = (rep + k) % replicas
            block = map_buf.at[m, pl.ds(pl.multiple_of(other * stored, stored), stored)]
            remote(block, block, map_send_sem.at[m, k], map_recv_sem.at[m, other], {"replica": other}).wait_recv()

    lane = lax.broadcasted_iota(jnp.int32, (rows, adapters * rank), 1)
    slot = jnp.concatenate([slots[...]] * (adapters * rank // 128), axis=1)
    pick = (lane >= slot * rank) & (lane < (slot + 1) * rank)

    def send_low(which, features):
        down = map_buf[2 * which].reshape(adapters * rank, width)
        part = lax.dot_general(features, down, (((1,), (1,)), ((), ())), preferred_element_type=F32)
        part = jnp.where(pick, part, 0.0)
        low_send[which] = sum(part[:, c : c + lanes] for c in range(0, adapters * rank, lanes))
        copies = []
        for k in range(1, tensor):
            copies.append(
                remote(
                    low_send.at[which],
                    low_recv.at[which, me],
                    low_send_sem.at[which, k],
                    low_recv_sem.at[which, me],
                    {"tensor": (me + k) % tensor},
                )
            )
            copies[-1].start()
        return copies

    def adapter_delta(which):
        total = low_send[which]
        for k in range(1, tensor):
            s = (me + k) % tensor
            remote(
                low_send.at[which], low_recv.at[which, s], low_send_sem.at[which, k], low_recv_sem.at[which, s], {"tensor": s}
            ).wait_recv()
            total = total + low_recv[which, s]
        spread = jnp.concatenate([total] * (adapters * rank // lanes), axis=1)
        spread = jnp.where(pick, spread, 0.0).astype(BF16)
        up = map_buf[2 * which + 1].reshape(adapters * rank, width)
        return 0.5 * jnp.dot(spread, up, preferred_element_type=F32)

    def wait_hidden(s):
        remote(h_buf.at[s], h_buf.at[s], h_send_sem.at[0], h_recv_sem.at[s], {"tensor": at(0, 1)}).wait_recv()

    wait_map(0)
    low_copies = send_low(0, h_buf[me])

    def add_chunk(s):
        wq_copy(s).wait()
        acc[...] += jnp.dot(h_buf[s], wq_buf[s], preferred_element_type=F32)

    acc[...] = jnp.zeros_like(acc)

    def forward(k):
        s = at(k, 0)
        return remote(h_buf.at[s], h_buf.at[s], fwd_send_sem.at[k], h_recv_sem.at[s], {"tensor": at(0, 1)})

    def near(k):
        s = at(k, 0)

        @pl.when(k > 0)
        def _():
            wait_hidden(s)
            if inner == 2:
                forward(k).start()

        add_chunk(s)

    def across(k):
        s = at(k, 1)
        wait_hidden(s)
        add_chunk(s)

    loop(outer, near)
    if inner == 2:
        loop(outer, across)

    wait_map(1)
    query = acc[...] + adapter_delta(0)

    for copy in kv_copies:
        copy.wait()
    per_kv = local_heads // kv_count
    shape = (per_kv * ROW_BLOCK, ROW_BLOCK * length)
    row = lax.broadcasted_iota(jnp.int32, shape, 0) % ROW_BLOCK
    column = lax.broadcasted_iota(jnp.int32, shape, 1)
    position = column - row * length
    for j in range(kv_count):
        for b in range(0, rows, ROW_BLOCK):
            heads = [
                query[b : b + ROW_BLOCK, h * head_size : (h + 1) * head_size]
                for h in range(j * per_kv, (j + 1) * per_kv)
            ]
            q = jnp.concatenate(heads, axis=0).astype(BF16)
            key = key_buf[j, b : b + ROW_BLOCK].reshape(ROW_BLOCK * length, head_size)
            value = value_buf[j, b : b + ROW_BLOCK].reshape(ROW_BLOCK * length, head_size)
            live = jnp.concatenate([lengths[b : b + ROW_BLOCK, 0:1]] * per_kv, axis=0)
            scores = lax.dot_general(q, key, (((1,), (1,)), ((), ())), preferred_element_type=F32)
            scores = scores * (1.0 / math.sqrt(head_size))
            scores = jnp.where((position >= 0) & (position < live), scores, -1e30)
            top = jnp.max(scores, axis=1, keepdims=True)
            weights = jnp.exp(scores - top)
            probs = (weights / jnp.sum(weights, axis=1, keepdims=True)).astype(BF16)
            result = jnp.dot(probs, value, preferred_element_type=F32)
            for n in range(per_kv):
                h = j * per_kv + n
                mixed[b : b + ROW_BLOCK, h * head_size : (h + 1) * head_size] = result[
                    n * ROW_BLOCK : (n + 1) * ROW_BLOCK
                ]

    features = mixed[...].astype(BF16)
    wait_map(2)
    low_copies += send_low(1, features)

    def pair_copy(k):
        d = (o + k) % outer
        return remote(
            pair_send.at[k], pair_recv.at[d], pair_send_sem.at[k], pair_recv_sem.at[d], {"tensor": at(0, 1)}
        )

    def far_copy(k):
        return remote(far_send.at[k], far_recv.at[o], far_send_sem.at[k], far_recv_sem.at[o], {"tensor": at(k, 0)})

    def product(s):
        ow_copy(s).wait()
        return jnp.dot(features, ow_buf[s], preferred_element_type=F32)

    def to_pair(n):
        k = (n + 1) % outer
        pair_send[k] = product(at(k, 1)).astype(BF16)
        pair_copy(k).start()

    if inner == 2:
        loop(outer, to_pair)

    def own_sum(k):
        total = product(at(k, 0))
        if inner == 2:
            pair_copy(k).wait_recv()
            total = total + pair_recv[(o + k) % outer].astype(F32)
        return total

    def to_far(k):
        far_send[k] = own_sum(k).astype(BF16)
        far_copy(k).start()

    loop(outer, to_far, 1)
    total = own_sum(0)
    wait_map(3)
    total = total + adapter_delta(1)
    for k in range(1, outer):
        s = (o + k) % outer
        remote(far_send.at[k], far_recv.at[s], far_send_sem.at[k], far_recv_sem.at[s], {"tensor": at(k, 0)}).wait_recv()
        total = total + far_recv[s].astype(F32)
    out[...] = total.astype(BF16)

    for copy in h_sends + map_copies + low_copies:
        copy.wait_send()
    for k in range(outer):
        if k > 0:
            far_copy(k).wait_send()
        if inner == 2:
            pair_copy(k).wait_send()
            if k > 0:
                forward(k).wait_send()


def per_device(tensor, replicas, *args):
    (
        hidden,
        w_query,
        output_weight,
        keys,
        values,
        query_down,
        query_up,
        output_down,
        output_up,
        adapter_ids,
        owner_map,
        kv_lengths,
    ) = args
    rows, width = hidden.shape
    cols = w_query.shape[1]
    stored, rank, _ = query_down.shape
    length, head_size = keys.shape[2:]
    replica_at = lax.axis_index("replica")
    own_ids = lax.dynamic_slice_in_dim(adapter_ids, replica_at * rows, rows)
    id_table = lax.broadcasted_iota(jnp.int32, (1, owner_map.shape[0]), 1)
    own_slots = jnp.sum(jnp.where(own_ids[:, None] == id_table, owner_map[None, :], 0), axis=1)
    slots = jnp.broadcast_to(own_slots[:, None], (rows, 128))
    lengths = jnp.broadcast_to(kv_lengths[:, None], (rows, 128))
    kv_count = max(1, cols // head_size // (HEADS // KVS))
    inner = 2 if tensor % 2 == 0 else 1
    outer = tensor // inner
    lanes = max(128, rank)
    dma = pltpu.SemaphoreType.DMA
    any_spec = pl.BlockSpec(memory_space=pl.ANY)
    vmem_spec = pl.BlockSpec(memory_space=pltpu.VMEM)
    return pl.pallas_call(
        functools.partial(block_kernel, tensor, replicas),
        out_shape=jax.ShapeDtypeStruct((rows, width), BF16),
        in_specs=[any_spec] * 9 + [vmem_spec] * 2,
        out_specs=vmem_spec,
        scratch_shapes=[
            pltpu.VMEM((tensor, rows, width), BF16),
            pltpu.VMEM((tensor, width, cols), BF16),
            pltpu.VMEM((tensor, cols, width), BF16),
            pltpu.VMEM((kv_count, rows, length, head_size), BF16),
            pltpu.VMEM((kv_count, rows, length, head_size), BF16),
            pltpu.VMEM((4, replicas * stored, rank, width), BF16),
            pltpu.VMEM((rows, cols), F32),
            pltpu.VMEM((rows, cols), F32),
            pltpu.VMEM((2, rows, lanes), F32),
            pltpu.VMEM((2, tensor, rows, lanes), F32),
            pltpu.VMEM((outer, rows, width), BF16),
            pltpu.VMEM((outer, rows, width), BF16),
            pltpu.VMEM((outer, rows, width), BF16),
            pltpu.VMEM((outer, rows, width), BF16),
            dma,
            dma((tensor,)),
            dma((tensor,)),
            dma((2, kv_count)),
            dma((4,)),
            dma((4, replicas)),
            dma((4, replicas)),
            dma((outer,)),
            dma((tensor,)),
            dma((outer,)),
            dma((2, tensor)),
            dma((2, tensor)),
            dma((outer,)),
            dma((outer,)),
            dma((outer,)),
            dma((outer,)),
        ],
        compiler_params=pltpu.CompilerParams(
            collective_id=0, has_side_effects=True, vmem_limit_bytes=58 * 1024 * 1024
        ),
    )(
        hidden,
        w_query,
        output_weight,
        keys,
        values,
        query_down,
        query_up,
        output_down,
        output_up,
        slots,
        lengths,
    )


def solution(mesh):
    return jax.shard_map(
        functools.partial(per_device, mesh.shape["tensor"], mesh.shape["replica"]),
        mesh=mesh,
        in_specs=(
            P(("groups", "replica"), "tensor"),
            P(None, "tensor"),
            P("tensor", None),
            P(("groups", "replica"), None, None, None),
            P(("groups", "replica"), None, None, None),
            P(("groups", "replica"), None, "tensor"),
            P(("groups", "replica"), None, "tensor"),
            P(("groups", "replica"), None, "tensor"),
            P(("groups", "replica"), None, "tensor"),
            P("groups"),
            P("groups"),
            P(("groups", "replica")),
        ),
        out_specs=P(("groups", "replica"), "tensor"),
        check_vma=False,
    )
```

```python
import functools
import math

import jax
import jax.numpy as jnp
from jax import lax
from jax.experimental import pallas as pl
from jax.experimental.pallas import tpu as pltpu
from jax.sharding import PartitionSpec as P

HEADS = 64
KVS = 8
ROW_BLOCK = 8
F32 = jnp.float32
BF16 = jnp.bfloat16


def loop(count, body, first=0):
    def step(k, carry):
        body(k)
        return carry

    if count > first:
        lax.fori_loop(first, count, step, 0)


def remote(src, dst, send_sem, recv_sem, device):
    return pltpu.make_async_remote_copy(
        src_ref=src,
        dst_ref=dst,
        send_sem=send_sem,
        recv_sem=recv_sem,
        device_id=device,
        device_id_type=pl.DeviceIdType.MESH,
    )


def block_kernel(
    tensor,
    replicas,
    hidden,
    w_query,
    output_weight,
    keys,
    values,
    query_down,
    query_up,
    output_down,
    output_up,
    ids,
    owners,
    lengths,
    out,
    h_buf,
    wq_buf,
    ow_buf,
    key_buf,
    value_buf,
    down_buf,
    qup_buf,
    oup_buf,
    len_buf,
    acc,
    mixed,
    mix_buf,
    low_send,
    low_recv,
    low_all,
    pair_send,
    pair_recv,
    far_send,
    far_recv,
    h_local,
    wq_sem,
    ow_sem,
    kv_sem,
    kv_send_sem,
    kv_recv_sem,
    map_local,
    map_send_sem,
    map_recv_sem,
    len_send_sem,
    len_recv_sem,
    h_send_sem,
    h_recv_sem,
    core_send_sem,
    fwd_send_sem,
    low_send_sem,
    low_recv_sem,
    all_send_sem,
    all_recv_sem,
    mix_send_sem,
    mix_recv_sem,
    pair_send_sem,
    pair_recv_sem,
    far_send_sem,
    far_recv_sem,
):
    rows, width = hidden.shape
    head_size = keys.shape[3]
    length = keys.shape[2]
    stored, rank, _ = query_down.shape
    adapters = stored * replicas
    half = wq_buf.shape[2]
    cols = half * replicas
    out_half = ow_buf.shape[2]
    every = replicas * rows
    lanes = low_send.shape[2]
    inner = 2 if tensor % 2 == 0 else 1
    outer = tensor // inner
    me = lax.axis_index("tensor")
    rep = lax.axis_index("replica")
    o, i = me // inner, me % inner

    def at(k, j):
        return ((o + k) % outer) * inner + (i + j) % inner

    def mate(q):
        return (rep + q) % replicas

    barrier = pltpu.get_barrier_semaphore()

    def greet(device):
        pl.semaphore_signal(barrier, inc=1, device_id=device, device_id_type=pl.DeviceIdType.MESH)

    for k in range(1, tensor):
        greet({"tensor": (me + k) % tensor})
    for q in range(1, replicas):
        for k in range(outer):
            greet({"tensor": at(k, 0), "replica": mate(q)})

    own_hidden = pltpu.make_async_copy(hidden, h_buf.at[me, rep], h_local)
    own_hidden.start()

    def block(index, size):
        return pl.ds(pl.multiple_of(index * size, size), size)

    def map_views(m, source, target):
        slots = block(source, stored)
        if m == 0:
            return query_down, down_buf.at[0, slots]
        if m == 1:
            return query_up.at[:, :, block(target, half)], qup_buf.at[slots]
        if m == 2:
            return output_down, down_buf.at[1, slots]
        return output_up, oup_buf.at[slots]

    def own_map(m):
        return pltpu.make_async_copy(*map_views(m, rep, rep), map_local.at[m])

    own_map(0).start()

    def wq_copy(s):
        return pltpu.make_async_copy(
            w_query.at[block(s, width), block(rep, half)], wq_buf.at[s], wq_sem.at[s]
        )

    def ow_copy(s):
        return pltpu.make_async_copy(
            output_weight.at[:, block(s * replicas + rep, out_half)], ow_buf.at[s], ow_sem.at[s]
        )

    def shard(n):
        return ((o + outer - n % outer) % outer) * inner + (i + n // outer) % inner

    for n in range(tensor):
        wq_copy(shard(n)).start()

    half_heads = half // head_size
    group = HEADS // KVS
    kv_count = key_buf.shape[0]
    per_kv = half_heads // kv_count

    def kv_copy(j, which, q):
        target = mate(q)
        head = (me * replicas + target) * half_heads // group + j
        source = (keys, values)[which].at[:, head]
        place = (key_buf, value_buf)[which].at[j, rep]
        if q == 0:
            return pltpu.make_async_copy(source, place, kv_sem.at[which, j])
        return remote(
            source, place, kv_send_sem.at[which, j, q], kv_recv_sem.at[which, j, rep], {"replica": target}
        )

    len_buf[rep] = jnp.zeros(len_buf.shape[1:], jnp.int32)
    len_buf[rep, :, 0:rows] = jnp.broadcast_to(lengths[...], (len_buf.shape[1], rows))

    pl.semaphore_wait(barrier, tensor - 1 + (replicas - 1) * outer)
    own_hidden.wait()

    sends = []

    def to_core(s, q):
        return remote(
            h_buf.at[s, rep], h_buf.at[s, rep], core_send_sem.at[s, q], h_recv_sem.at[s, rep], {"replica": mate(q)}
        )

    def to_inner(s, k):
        return remote(
            h_buf.at[s, rep], h_buf.at[s, rep], fwd_send_sem.at[k], h_recv_sem.at[s, rep], {"tensor": at(0, 1)}
        )

    for k in range(1, outer):
        sends.append(
            remote(
                h_buf.at[me, rep],
                h_buf.at[me, rep],
                h_send_sem.at[k],
                h_recv_sem.at[me, rep],
                {"tensor": at(k, 0)},
            )
        )
    if inner == 2:
        sends.append(to_inner(me, 0))
    for q in range(1, replicas):
        sends.append(to_core(me, q))

    def map_copy(m, q):
        source, place = map_views(m, rep, mate(q))
        return remote(
            source, place, map_send_sem.at[m, q], map_recv_sem.at[m, rep], {"replica": mate(q)}
        )

    for m in range(4):
        for q in range(1, replicas):
            sends.append(map_copy(m, q))
            if m == 1:
                for j in range(kv_count):
                    sends += [kv_copy(j, 0, q), kv_copy(j, 1, q)]
                sends.append(
                    remote(
                        len_buf.at[rep],
                        len_buf.at[rep],
                        len_send_sem.at[q],
                        len_recv_sem.at[rep],
                        {"replica": mate(q)},
                    )
                )
    for copy in sends:
        copy.start()
    for m in range(1, 4):
        own_map(m).start()
    for j in range(kv_count):
        kv_copy(j, 0, 0).start()
        kv_copy(j, 1, 0).start()
    for j in reversed(range(inner)):
        for k in list(range(1, outer)) + [0]:
            ow_copy(at(k, j)).start()

    def arrived(place, sem):
        remote(place, place, h_send_sem.at[0], sem, {"replica": mate(1)}).wait_recv()

    def wait_map(m):
        own_map(m).wait()
        for q in range(1, replicas):
            _, place = map_views(m, mate(q), rep)
            arrived(place, map_recv_sem.at[m, mate(q)])

    def down_rows(line, count, first):
        size = line.shape[1]
        row = lax.broadcasted_iota(jnp.int32, (count, size), 0) + first
        column = lax.broadcasted_iota(jnp.int32, (count, size), 1)
        return jnp.sum(jnp.where(row == column, line, 0.0), axis=1, keepdims=True)

    def picks(count, first):
        own_ids = down_rows(ids[...].astype(F32), count, first)
        table = lax.broadcasted_iota(jnp.int32, (count, adapters), 1).astype(F32)
        slot = jnp.sum(jnp.where(own_ids == table, owners[...].astype(F32), 0.0), axis=1, keepdims=True)
        lane = lax.broadcasted_iota(jnp.int32, (count, adapters * rank), 1) // rank
        return lane.astype(F32) == slot

    own_pick = picks(rows, rep * rows)

    def send_low(which, features):
        down = down_buf[which].reshape(adapters * rank, width)
        part = lax.dot_general(features, down, (((1,), (1,)), ((), ())), preferred_element_type=F32)
        part = jnp.where(own_pick, part, 0.0)
        low_send[which] = sum(part[:, c : c + lanes] for c in range(0, adapters * rank, lanes))
        for k in range(1, tensor):
            sends.append(
                remote(
                    low_send.at[which],
                    low_recv.at[which, me],
                    low_send_sem.at[which, k],
                    low_recv_sem.at[which, me],
                    {"tensor": (me + k) % tensor},
                )
            )
            sends[-1].start()

    def low_total(which):
        total = low_send[which]
        for k in range(1, tensor):
            s = (me + k) % tensor
            arrived(low_recv.at[which, s], low_recv_sem.at[which, s])
            total = total + low_recv[which, s]
        return total

    def adapter_delta(total, pick, up):
        spread = jnp.concatenate([total] * (adapters * rank // lanes), axis=1)
        spread = jnp.where(pick, spread, 0.0).astype(BF16)
        return 0.5 * jnp.dot(spread, up, preferred_element_type=F32)

    wait_map(0)
    send_low(0, h_buf[me, rep])
    acc[...] = jnp.zeros_like(acc)

    def use_shard(n):
        s = shard(n)
        following = shard(n + 1)

        @pl.when(n + 1 < tensor)
        def _():
            arrived(h_buf.at[following, rep], h_recv_sem.at[following, rep])
            for q in range(1, replicas):
                to_core(following, q).start()

        if inner == 2:

            @pl.when(n + 1 < outer)
            def _():
                to_inner(following, n + 1).start()

        wq_copy(s).wait()
        for q in range(1, replicas):
            arrived(h_buf.at[s, mate(q)], h_recv_sem.at[s, mate(q)])
        acc[...] += jnp.dot(h_buf[s].reshape(every, width), wq_buf[s], preferred_element_type=F32)

    loop(outer, use_shard)
    low_all[rep] = low_total(0)
    for q in range(1, replicas):
        sends.append(
            remote(
                low_all.at[rep], low_all.at[rep], all_send_sem.at[q], all_recv_sem.at[rep], {"replica": mate(q)}
            )
        )
        sends[-1].start()
    loop(tensor, use_shard, outer)

    wait_map(1)
    for q in range(1, replicas):
        arrived(low_all.at[mate(q)], all_recv_sem.at[mate(q)])
    query = acc[...] + adapter_delta(
        low_all[...].reshape(every, lanes),
        picks(every, 0),
        qup_buf[...].reshape(adapters * rank, half),
    )

    for j in range(kv_count):
        for which in range(2):
            kv_copy(j, which, 0).wait()
            for q in range(1, replicas):
                place = (key_buf, value_buf)[which].at[j, mate(q)]
                arrived(place, kv_recv_sem.at[which, j, mate(q)])
    for q in range(1, replicas):
        arrived(len_buf.at[mate(q)], len_recv_sem.at[mate(q)])
    shape = (per_kv * ROW_BLOCK, ROW_BLOCK * length)
    row = lax.broadcasted_iota(jnp.int32, shape, 0) % ROW_BLOCK
    column = lax.broadcasted_iota(jnp.int32, shape, 1)
    position = (column - row * length).astype(F32)
    for r in range(replicas):
        held = down_rows(len_buf[r, 0:1].astype(F32), rows, 0)
        for j in range(kv_count):
            for b in range(0, rows, ROW_BLOCK):
                at_row = r * rows + b
                heads = [
                    query[at_row : at_row + ROW_BLOCK, h * head_size : (h + 1) * head_size]
                    for h in range(j * per_kv, (j + 1) * per_kv)
                ]
                q = jnp.concatenate(heads, axis=0).astype(BF16)
                key = key_buf[j, r, b : b + ROW_BLOCK].reshape(ROW_BLOCK * length, head_size)
                value = value_buf[j, r, b : b + ROW_BLOCK].reshape(ROW_BLOCK * length, head_size)
                live = jnp.concatenate([held[b : b + ROW_BLOCK]] * per_kv, axis=0)
                scores = lax.dot_general(q, key, (((1,), (1,)), ((), ())), preferred_element_type=F32)
                scores = scores * (1.0 / math.sqrt(head_size))
                scores = jnp.where((position >= 0) & (position < live), scores, -1e30)
                top = jnp.max(scores, axis=1, keepdims=True)
                weights = jnp.exp(scores - top)
                probs = (weights / jnp.sum(weights, axis=1, keepdims=True)).astype(BF16)
                result = jnp.dot(probs, value, preferred_element_type=F32)
                for n in range(per_kv):
                    h = j * per_kv + n
                    mixed[at_row : at_row + ROW_BLOCK, h * head_size : (h + 1) * head_size] = result[
                        n * ROW_BLOCK : (n + 1) * ROW_BLOCK
                    ]

    mix_buf[rep] = mixed[...].astype(BF16)
    for q in range(1, replicas):
        sends.append(
            remote(
                mix_buf.at[rep], mix_buf.at[rep], mix_send_sem.at[q], mix_recv_sem.at[rep], {"replica": mate(q)}
            )
        )
        sends[-1].start()
    wait_map(2)
    wait_map(3)
    for q in range(1, replicas):
        arrived(mix_buf.at[mate(q)], mix_recv_sem.at[mate(q)])

    def pair_copy(k):
        d = (o + k) % outer
        return remote(
            pair_send.at[k], pair_recv.at[d], pair_send_sem.at[k], pair_recv_sem.at[d], {"tensor": at(0, 1)}
        )

    def far_copy(k, q):
        target = mate(q)
        return remote(
            far_send.at[k, target],
            far_recv.at[o, rep],
            far_send_sem.at[k, q],
            far_recv_sem.at[o, rep],
            {"tensor": at(k, 0), "replica": target},
        )

    def product(s):
        ow_copy(s).wait()
        features = jnp.concatenate([mix_buf[r] for r in range(replicas)], axis=1)
        return jnp.dot(features, ow_buf[s], preferred_element_type=F32)

    def to_pair(n):
        k = (n + 1) % outer
        pair_send[k] = product(at(k, 1)).astype(BF16)
        pair_copy(k).start()

    if inner == 2:
        loop(outer, to_pair)

    own_rows = block(rep, rows)
    send_low(1, jnp.concatenate([mix_buf[r, own_rows] for r in range(replicas)], axis=1))

    def to_far(n):
        k = (n + 1) % outer
        total = product(at(k, 0))
        if inner == 2:
            d = (o + k) % outer
            arrived(pair_recv.at[d], pair_recv_sem.at[d])
            total = total + pair_recv[d].astype(F32)
        for r in range(replicas):
            far_send[k, r] = total[r * rows : (r + 1) * rows].astype(BF16)
        for q in range(1, replicas):
            far_copy(k, q).start()

        @pl.when(k > 0)
        def _():
            far_copy(k, 0).start()

    loop(outer, to_far)
    far_recv[o, rep] = far_send[0, rep]
    delta = adapter_delta(low_total(1), own_pick, oup_buf[...].reshape(adapters * rank, width))
    sums = [delta[:, r * out_half : (r + 1) * out_half] for r in range(replicas)]
    for k in range(outer):
        for q in range(replicas):
            if k > 0 or q > 0:
                s, r = (o + k) % outer, mate(q)
                arrived(far_recv.at[s, r], far_recv_sem.at[s, r])
    for r in range(replicas):
        for s in range(outer):
            sums[r] = sums[r] + far_recv[s, r].astype(F32)
        out[:, r * out_half : (r + 1) * out_half] = sums[r].astype(BF16)

    for copy in sends:
        copy.wait_send()
    for k in range(outer):
        for q in range(replicas):
            if k > 0 or q > 0:
                far_copy(k, q).wait_send()
        if inner == 2:
            pair_copy(k).wait_send()
            if k > 0:
                to_inner(shard(k), k).wait_send()
    for n in range(1, tensor):
        for q in range(1, replicas):
            to_core(shard(n), q).wait_send()


def per_device(tensor, replicas, *args):
    (
        hidden,
        w_query,
        output_weight,
        keys,
        values,
        query_down,
        query_up,
        output_down,
        output_up,
        adapter_ids,
        owner_map,
        kv_lengths,
    ) = args
    rows, width = hidden.shape
    cols = w_query.shape[1]
    stored, rank, _ = query_down.shape
    length, head_size = keys.shape[2:]
    half, out_half = cols // replicas, width // replicas
    every, adapters = replicas * rows, replicas * stored
    kv_count = max(1, half // head_size // (HEADS // KVS))
    inner = 2 if tensor % 2 == 0 else 1
    outer = tensor // inner
    lanes = max(128, rank)
    dma = pltpu.SemaphoreType.DMA
    any_spec = pl.BlockSpec(memory_space=pl.ANY)
    vmem_spec = pl.BlockSpec(memory_space=pltpu.VMEM)
    return pl.pallas_call(
        functools.partial(block_kernel, tensor, replicas),
        out_shape=jax.ShapeDtypeStruct((rows, width), BF16),
        in_specs=[any_spec] * 9 + [vmem_spec] * 3,
        out_specs=vmem_spec,
        scratch_shapes=[
            pltpu.VMEM((tensor, replicas, rows, width), BF16),
            pltpu.VMEM((tensor, width, half), BF16),
            pltpu.VMEM((tensor, cols, out_half), BF16),
            pltpu.VMEM((kv_count, replicas, rows, length, head_size), BF16),
            pltpu.VMEM((kv_count, replicas, rows, length, head_size), BF16),
            pltpu.VMEM((2, adapters, rank, width), BF16),
            pltpu.VMEM((adapters, rank, half), BF16),
            pltpu.VMEM((adapters, rank, width), BF16),
            pltpu.VMEM((replicas, 8, 128), jnp.int32),
            pltpu.VMEM((every, half), F32),
            pltpu.VMEM((every, half), F32),
            pltpu.VMEM((replicas, every, half), BF16),
            pltpu.VMEM((2, rows, lanes), F32),
            pltpu.VMEM((2, tensor, rows, lanes), F32),
            pltpu.VMEM((replicas, rows, lanes), F32),
            pltpu.VMEM((outer, every, out_half), BF16),
            pltpu.VMEM((outer, every, out_half), BF16),
            pltpu.VMEM((outer, replicas, rows, out_half), BF16),
            pltpu.VMEM((outer, replicas, rows, out_half), BF16),
            dma,
            dma((tensor,)),
            dma((tensor,)),
            dma((2, kv_count)),
            dma((2, kv_count, replicas)),
            dma((2, kv_count, replicas)),
            dma((4,)),
            dma((4, replicas)),
            dma((4, replicas)),
            dma((replicas,)),
            dma((replicas,)),
            dma((outer,)),
            dma((tensor, replicas)),
            dma((tensor, replicas)),
            dma((outer,)),
            dma((2, tensor)),
            dma((2, tensor)),
            dma((replicas,)),
            dma((replicas,)),
            dma((replicas,)),
            dma((replicas,)),
            dma((outer,)),
            dma((outer,)),
            dma((outer, replicas)),
            dma((outer, replicas)),
        ],
        compiler_params=pltpu.CompilerParams(
            collective_id=0, has_side_effects=True, vmem_limit_bytes=58 * 1024 * 1024
        ),
    )(
        hidden,
        w_query,
        output_weight,
        keys,
        values,
        query_down,
        query_up,
        output_down,
        output_up,
        adapter_ids.reshape(1, -1),
        owner_map.reshape(1, -1),
        kv_lengths.reshape(1, -1),
    )


def solution(mesh):
    return jax.shard_map(
        functools.partial(per_device, mesh.shape["tensor"], mesh.shape["replica"]),
        mesh=mesh,
        in_specs=(
            P(("groups", "replica"), "tensor"),
            P(None, "tensor"),
            P("tensor", None),
            P(("groups", "replica"), None, None, None),
            P(("groups", "replica"), None, None, None),
            P(("groups", "replica"), None, "tensor"),
            P(("groups", "replica"), None, "tensor"),
            P(("groups", "replica"), None, "tensor"),
            P(("groups", "replica"), None, "tensor"),
            P("groups"),
            P("groups"),
            P(("groups", "replica")),
        ),
        out_specs=P(("groups", "replica"), "tensor"),
        check_vma=False,
    )
```

```python
import functools
import math

import jax
import jax.numpy as jnp
from jax import lax
from jax.experimental import pallas as pl
from jax.experimental.pallas import tpu as pltpu
from jax.sharding import PartitionSpec as P

HEADS = 64
KVS = 8
ROW_BLOCK = 8
F32 = jnp.float32
BF16 = jnp.bfloat16


def loop(count, body, first=0):
    def step(k, carry):
        body(k)
        return carry

    if count > first:
        lax.fori_loop(first, count, step, 0)


def remote(src, dst, send_sem, recv_sem, device):
    return pltpu.make_async_remote_copy(
        src_ref=src,
        dst_ref=dst,
        send_sem=send_sem,
        recv_sem=recv_sem,
        device_id=device,
        device_id_type=pl.DeviceIdType.MESH,
    )


def block_kernel(
    tensor,
    replicas,
    hidden,
    w_query,
    output_weight,
    keys,
    values,
    query_down,
    query_up,
    output_down,
    output_up,
    ids,
    owners,
    lengths,
    out,
    h_buf,
    wq_buf,
    ow_buf,
    key_buf,
    value_buf,
    down_buf,
    qup_buf,
    oup_buf,
    len_buf,
    acc,
    mixed,
    mix_buf,
    low_send,
    low_recv,
    spread_buf,
    delta_send,
    delta_recv,
    pair_send,
    pair_recv,
    far_send,
    far_recv,
    h_local,
    wq_sem,
    ow_sem,
    kv_sem,
    kv_send_sem,
    kv_recv_sem,
    map_local,
    delta_send_sem,
    delta_recv_sem,
    len_send_sem,
    len_recv_sem,
    h_send_sem,
    h_recv_sem,
    core_send_sem,
    fwd_send_sem,
    low_send_sem,
    low_recv_sem,
    mix_send_sem,
    mix_recv_sem,
    pair_send_sem,
    pair_recv_sem,
    far_send_sem,
    far_recv_sem,
):
    rows, width = hidden.shape
    head_size = keys.shape[3]
    length = keys.shape[2]
    stored, rank, _ = query_down.shape
    half = wq_buf.shape[2]
    cols = half * replicas
    out_half = ow_buf.shape[2]
    every = replicas * rows
    lanes = low_send.shape[2]
    packed = lanes // rank
    inner = 2 if tensor % 2 == 0 else 1
    outer = tensor // inner
    me = lax.axis_index("tensor")
    rep = lax.axis_index("replica")
    o, i = me // inner, me % inner

    def at(k, j):
        return ((o + k) % outer) * inner + (i + j) % inner

    def mate(q):
        return (rep + q) % replicas

    barrier = pltpu.get_barrier_semaphore()

    def greet(device):
        pl.semaphore_signal(barrier, inc=1, device_id=device, device_id_type=pl.DeviceIdType.MESH)

    for k in range(1, tensor):
        greet({"tensor": (me + k) % tensor})
    for q in range(1, replicas):
        for k in range(outer):
            greet({"tensor": at(k, 0), "replica": mate(q)})

    own_hidden = pltpu.make_async_copy(hidden, h_buf.at[me, rep], h_local)
    own_hidden.start()

    def block(index, size):
        return pl.ds(pl.multiple_of(index * size, size), size)

    def map_copies(m):
        if m % 2 == 0:
            source = (query_down, output_down)[m // 2]
            return [pltpu.make_async_copy(source, down_buf.at[m // 2], map_local.at[m, 0])]
        source, place = ((query_up, qup_buf), (output_up, oup_buf))[m // 2]
        size = place.shape[3]
        return [
            pltpu.make_async_copy(source.at[:, :, r * size : (r + 1) * size], place.at[r], map_local.at[m, r])
            for r in range(replicas)
        ]

    def start_map(m):
        for copy in map_copies(m):
            copy.start()

    def wait_map(m):
        for copy in map_copies(m):
            copy.wait()

    start_map(0)

    def wq_copy(s):
        return pltpu.make_async_copy(
            w_query.at[block(s, width), block(rep, half)], wq_buf.at[s], wq_sem.at[s]
        )

    def ow_copy(s):
        return pltpu.make_async_copy(
            output_weight.at[:, block(s * replicas + rep, out_half)], ow_buf.at[s], ow_sem.at[s]
        )

    def shard(n):
        return ((o + outer - n % outer) % outer) * inner + (i + n // outer) % inner

    def target(n):
        return at((n + 1) % outer, inner - 1 - n // outer)

    ahead = min(3, tensor)
    for n in range(ahead):
        wq_copy(shard(n)).start()

    half_heads = half // head_size
    group = HEADS // KVS
    kv_count = key_buf.shape[0]
    per_kv = half_heads // kv_count

    def kv_copy(j, which, q):
        target = mate(q)
        head = (me * replicas + target) * half_heads // group + j
        source = (keys, values)[which].at[:, head]
        place = (key_buf, value_buf)[which].at[j, rep]
        if q == 0:
            return pltpu.make_async_copy(source, place, kv_sem.at[which, j])
        return remote(
            source, place, kv_send_sem.at[which, j, q], kv_recv_sem.at[which, j, rep], {"replica": target}
        )

    len_buf[rep] = jnp.zeros(len_buf.shape[1:], jnp.int32)
    len_buf[rep, :, 0:rows] = jnp.broadcast_to(lengths[...], (len_buf.shape[1], rows))

    pl.semaphore_wait(barrier, tensor - 1 + (replicas - 1) * outer)
    own_hidden.wait()

    sends = []

    def to_core(s, q):
        return remote(
            h_buf.at[s, rep], h_buf.at[s, rep], core_send_sem.at[s, q], h_recv_sem.at[s, rep], {"replica": mate(q)}
        )

    def to_inner(s, k):
        return remote(
            h_buf.at[s, rep], h_buf.at[s, rep], fwd_send_sem.at[k], h_recv_sem.at[s, rep], {"tensor": at(0, 1)}
        )

    for k in range(1, outer):
        sends.append(
            remote(
                h_buf.at[me, rep],
                h_buf.at[me, rep],
                h_send_sem.at[k],
                h_recv_sem.at[me, rep],
                {"tensor": at(k, 0)},
            )
        )
    if inner == 2:
        sends.append(to_inner(me, 0))
    for q in range(1, replicas):
        sends.append(to_core(me, q))

    for copy in sends:
        copy.start()
    late = []
    for q in range(1, replicas):
        for j in range(kv_count):
            late += [kv_copy(j, 0, q), kv_copy(j, 1, q)]
        late.append(
            remote(len_buf.at[rep], len_buf.at[rep], len_send_sem.at[q], len_recv_sem.at[rep], {"replica": mate(q)})
        )

    def arrived(place, sem):
        remote(place, place, h_send_sem.at[0], sem, {"replica": mate(1)}).wait_recv()

    def down_rows(line, count, first):
        size = line.shape[1]
        row = lax.broadcasted_iota(jnp.int32, (count, size), 0) + first
        column = lax.broadcasted_iota(jnp.int32, (count, size), 1)
        return jnp.sum(jnp.where(row == column, line, 0.0), axis=1, keepdims=True)

    every_id = down_rows(ids[...].astype(F32), every, 0)
    table = lax.broadcasted_iota(jnp.int32, (every, owners.shape[1]), 1).astype(F32)
    slot = jnp.sum(jnp.where(every_id == table, owners[...].astype(F32), 0.0), axis=1, keepdims=True)
    lane = lax.broadcasted_iota(jnp.int32, (every, stored * rank), 1) // rank + rep * stored
    pick = lane.astype(F32) == slot
    lower = lax.broadcasted_iota(jnp.int32, (every // packed, lanes), 1) < rank

    def turned(x):
        return jnp.concatenate([x[:, rank:], x[:, :rank]], axis=1)

    def send_low(which, features):
        down = down_buf[which].reshape(stored * rank, width)
        part = lax.dot_general(features, down, (((1,), (1,)), ((), ())), preferred_element_type=F32)
        part = jnp.where(pick, part, 0.0)
        part = sum(part[:, c : c + lanes] for c in range(0, stored * rank, lanes))
        if packed == 2:
            part = part + turned(part)
            part = jnp.where(lower, part[: every // 2], part[every // 2 :])
        low_send[which] = part.astype(BF16)
        for k in range(1, tensor):
            sends.append(
                remote(
                    low_send.at[which],
                    low_recv.at[which, me],
                    low_send_sem.at[which, k],
                    low_recv_sem.at[which, me],
                    {"tensor": (me + k) % tensor},
                )
            )
            sends[-1].start()

    def spread_low(which):
        total = low_send[which].astype(F32)
        for k in range(1, tensor):
            s = (me + k) % tensor
            arrived(low_recv.at[which, s], low_recv_sem.at[which, s])
            total = total + low_recv[which, s].astype(F32)
        if packed == 2:
            other = turned(total)
            total = jnp.concatenate(
                [jnp.where(lower, total, other), jnp.where(lower, other, total)], axis=0
            )
        spread = jnp.concatenate([total] * (stored * rank // lanes), axis=1)
        return jnp.where(pick, spread, 0.0).astype(BF16)

    def delta_copy(which, q):
        return remote(
            delta_send.at[which, q],
            delta_recv.at[which, rep],
            delta_send_sem.at[which, q],
            delta_recv_sem.at[which, rep],
            {"replica": mate(q)},
        )

    acc[...] = jnp.zeros_like(acc)

    def use_shard(n):
        s = shard(n)
        following = shard(n + 1)

        @pl.when(n + 1 < tensor)
        def _():
            arrived(h_buf.at[following, rep], h_recv_sem.at[following, rep])
            for q in range(1, replicas):
                to_core(following, q).start()

        if inner == 2:

            @pl.when(n + 1 < outer)
            def _():
                to_inner(following, n + 1).start()

        @pl.when(n + ahead < tensor)
        def _():
            wq_copy(shard(n + ahead)).start()

        ow_copy(target(n)).start()
        wq_copy(s).wait()
        for q in range(1, replicas):
            arrived(h_buf.at[s, mate(q)], h_recv_sem.at[s, mate(q)])
        acc[...] += jnp.dot(h_buf[s].reshape(every, width), wq_buf[s], preferred_element_type=F32)

    first, second = tensor // 4, tensor * 3 // 4
    loop(first, use_shard)
    for copy in late:
        copy.start()
    for j in range(kv_count):
        kv_copy(j, 0, 0).start()
        kv_copy(j, 1, 0).start()
    for m in range(1, 4):
        start_map(m)
    wait_map(0)
    if first == 0:
        for q in range(1, replicas):
            arrived(h_buf.at[me, mate(q)], h_recv_sem.at[me, mate(q)])
    send_low(0, h_buf[me].reshape(every, width))
    loop(second, use_shard, first)

    wait_map(1)
    spread = spread_low(0)

    def query_delta(r):
        return 0.5 * jnp.dot(spread, qup_buf[r].reshape(stored * rank, half), preferred_element_type=F32)

    for q in range(1, replicas):
        delta_send[0, q] = query_delta(mate(q)).astype(BF16)
        sends.append(delta_copy(0, q))
        sends[-1].start()
    acc[...] += query_delta(rep)
    loop(tensor, use_shard, second)

    query = acc[...]
    for q in range(1, replicas):
        arrived(delta_recv.at[0, mate(q)], delta_recv_sem.at[0, mate(q)])
        query = query + delta_recv[0, mate(q)].astype(F32)

    for j in range(kv_count):
        for which in range(2):
            kv_copy(j, which, 0).wait()
            for q in range(1, replicas):
                place = (key_buf, value_buf)[which].at[j, mate(q)]
                arrived(place, kv_recv_sem.at[which, j, mate(q)])
    for q in range(1, replicas):
        arrived(len_buf.at[mate(q)], len_recv_sem.at[mate(q)])
    shape = (per_kv * ROW_BLOCK, ROW_BLOCK * length)
    row = lax.broadcasted_iota(jnp.int32, shape, 0) % ROW_BLOCK
    column = lax.broadcasted_iota(jnp.int32, shape, 1)
    position = (column - row * length).astype(F32)
    for r in range(replicas):
        held = down_rows(len_buf[r, 0:1].astype(F32), rows, 0)
        for j in range(kv_count):
            for b in range(0, rows, ROW_BLOCK):
                at_row = r * rows + b
                heads = [
                    query[at_row : at_row + ROW_BLOCK, h * head_size : (h + 1) * head_size]
                    for h in range(j * per_kv, (j + 1) * per_kv)
                ]
                q = jnp.concatenate(heads, axis=0).astype(BF16)
                key = key_buf[j, r, b : b + ROW_BLOCK].reshape(ROW_BLOCK * length, head_size)
                value = value_buf[j, r, b : b + ROW_BLOCK].reshape(ROW_BLOCK * length, head_size)
                live = jnp.concatenate([held[b : b + ROW_BLOCK]] * per_kv, axis=0)
                scores = lax.dot_general(q, key, (((1,), (1,)), ((), ())), preferred_element_type=F32)
                scores = scores * (1.0 / math.sqrt(head_size))
                scores = jnp.where((position >= 0) & (position < live), scores, -1e30)
                top = jnp.max(scores, axis=1, keepdims=True)
                weights = jnp.exp(scores - top)
                probs = (weights / jnp.sum(weights, axis=1, keepdims=True)).astype(BF16)
                result = jnp.dot(probs, value, preferred_element_type=F32)
                for n in range(per_kv):
                    h = j * per_kv + n
                    mixed[at_row : at_row + ROW_BLOCK, h * head_size : (h + 1) * head_size] = result[
                        n * ROW_BLOCK : (n + 1) * ROW_BLOCK
                    ]

    mix_buf[rep] = mixed[...].astype(BF16)
    for q in range(1, replicas):
        sends.append(
            remote(
                mix_buf.at[rep], mix_buf.at[rep], mix_send_sem.at[q], mix_recv_sem.at[rep], {"replica": mate(q)}
            )
        )
        sends[-1].start()
    wait_map(2)
    wait_map(3)
    for q in range(1, replicas):
        arrived(mix_buf.at[mate(q)], mix_recv_sem.at[mate(q)])

    def pair_copy(k):
        d = (o + k) % outer
        return remote(
            pair_send.at[k], pair_recv.at[d], pair_send_sem.at[k], pair_recv_sem.at[d], {"tensor": at(0, 1)}
        )

    def far_copy(k, q):
        target = mate(q)
        return remote(
            far_send.at[k, target],
            far_recv.at[o, rep],
            far_send_sem.at[k, q],
            far_recv_sem.at[o, rep],
            {"tensor": at(k, 0), "replica": target},
        )

    def product(s):
        ow_copy(s).wait()
        features = jnp.concatenate([mix_buf[r] for r in range(replicas)], axis=1)
        return jnp.dot(features, ow_buf[s], preferred_element_type=F32)

    def to_pair(n):
        k = (n + 1) % outer
        pair_send[k] = product(at(k, 1)).astype(BF16)
        pair_copy(k).start()

    if inner == 2:
        loop(outer, to_pair)

    send_low(1, jnp.concatenate([mix_buf[r] for r in range(replicas)], axis=1))

    def to_far(n):
        k = (n + 1) % outer
        total = product(at(k, 0))
        if inner == 2:
            d = (o + k) % outer
            arrived(pair_recv.at[d], pair_recv_sem.at[d])
            total = total + pair_recv[d].astype(F32)
        for r in range(replicas):
            far_send[k, r] = total[r * rows : (r + 1) * rows].astype(BF16)
        for q in range(1, replicas):
            far_copy(k, q).start()

        @pl.when(k > 0)
        def _():
            far_copy(k, 0).start()

    loop(outer, to_far)
    far_recv[o, rep] = far_send[0, rep]
    spread_buf[...] = spread_low(1).reshape(spread_buf.shape)

    def output_delta(r, c):
        return 0.5 * jnp.dot(
            spread_buf[r], oup_buf[c].reshape(stored * rank, out_half), preferred_element_type=F32
        )

    for q in range(1, replicas):
        for c in range(replicas):
            delta_send[1, q, c * rows : (c + 1) * rows] = output_delta(mate(q), c).astype(BF16)
        sends.append(delta_copy(1, q))
        sends[-1].start()
    sums = [output_delta(rep, c) for c in range(replicas)]
    for q in range(1, replicas):
        arrived(delta_recv.at[1, mate(q)], delta_recv_sem.at[1, mate(q)])
        for c in range(replicas):
            sums[c] = sums[c] + delta_recv[1, mate(q), c * rows : (c + 1) * rows].astype(F32)
    for k in range(outer):
        for q in range(replicas):
            if k > 0 or q > 0:
                s, r = (o + k) % outer, mate(q)
                arrived(far_recv.at[s, r], far_recv_sem.at[s, r])
    for r in range(replicas):
        for s in range(outer):
            sums[r] = sums[r] + far_recv[s, r].astype(F32)
        out[:, r * out_half : (r + 1) * out_half] = sums[r].astype(BF16)

    for copy in sends + late:
        copy.wait_send()
    for k in range(outer):
        for q in range(replicas):
            if k > 0 or q > 0:
                far_copy(k, q).wait_send()
        if inner == 2:
            pair_copy(k).wait_send()
            if k > 0:
                to_inner(shard(k), k).wait_send()
    for n in range(1, tensor):
        for q in range(1, replicas):
            to_core(shard(n), q).wait_send()


def per_device(tensor, replicas, *args):
    (
        hidden,
        w_query,
        output_weight,
        keys,
        values,
        query_down,
        query_up,
        output_down,
        output_up,
        adapter_ids,
        owner_map,
        kv_lengths,
    ) = args
    rows, width = hidden.shape
    cols = w_query.shape[1]
    stored, rank, _ = query_down.shape
    length, head_size = keys.shape[2:]
    half, out_half = cols // replicas, width // replicas
    every = replicas * rows
    kv_count = max(1, half // head_size // (HEADS // KVS))
    inner = 2 if tensor % 2 == 0 else 1
    outer = tensor // inner
    lanes = max(128, rank)
    dma = pltpu.SemaphoreType.DMA
    any_spec = pl.BlockSpec(memory_space=pl.ANY)
    vmem_spec = pl.BlockSpec(memory_space=pltpu.VMEM)
    return pl.pallas_call(
        functools.partial(block_kernel, tensor, replicas),
        out_shape=jax.ShapeDtypeStruct((rows, width), BF16),
        in_specs=[any_spec] * 9 + [vmem_spec] * 3,
        out_specs=vmem_spec,
        scratch_shapes=[
            pltpu.VMEM((tensor, replicas, rows, width), BF16),
            pltpu.VMEM((tensor, width, half), BF16),
            pltpu.VMEM((tensor, cols, out_half), BF16),
            pltpu.VMEM((kv_count, replicas, rows, length, head_size), BF16),
            pltpu.VMEM((kv_count, replicas, rows, length, head_size), BF16),
            pltpu.VMEM((2, stored, rank, width), BF16),
            pltpu.VMEM((replicas, stored, rank, half), BF16),
            pltpu.VMEM((replicas, stored, rank, out_half), BF16),
            pltpu.VMEM((replicas, 8, 128), jnp.int32),
            pltpu.VMEM((every, half), F32),
            pltpu.VMEM((every, half), F32),
            pltpu.VMEM((replicas, every, half), BF16),
            pltpu.VMEM((2, every * rank // lanes, lanes), BF16),
            pltpu.VMEM((2, tensor, every * rank // lanes, lanes), BF16),
            pltpu.VMEM((replicas, rows, stored * rank), BF16),
            pltpu.VMEM((2, replicas, every, half), BF16),
            pltpu.VMEM((2, replicas, every, half), BF16),
            pltpu.VMEM((outer, every, out_half), BF16),
            pltpu.VMEM((outer, every, out_half), BF16),
            pltpu.VMEM((outer, replicas, rows, out_half), BF16),
            pltpu.VMEM((outer, replicas, rows, out_half), BF16),
            dma,
            dma((tensor,)),
            dma((tensor,)),
            dma((2, kv_count)),
            dma((2, kv_count, replicas)),
            dma((2, kv_count, replicas)),
            dma((4, replicas)),
            dma((2, replicas)),
            dma((2, replicas)),
            dma((replicas,)),
            dma((replicas,)),
            dma((outer,)),
            dma((tensor, replicas)),
            dma((tensor, replicas)),
            dma((outer,)),
            dma((2, tensor)),
            dma((2, tensor)),
            dma((replicas,)),
            dma((replicas,)),
            dma((outer,)),
            dma((outer,)),
            dma((outer, replicas)),
            dma((outer, replicas)),
        ],
        compiler_params=pltpu.CompilerParams(
            collective_id=0, has_side_effects=True, vmem_limit_bytes=58 * 1024 * 1024
        ),
    )(
        hidden,
        w_query,
        output_weight,
        keys,
        values,
        query_down,
        query_up,
        output_down,
        output_up,
        adapter_ids.reshape(1, -1),
        owner_map.reshape(1, -1),
        kv_lengths.reshape(1, -1),
    )


def solution(mesh):
    return jax.shard_map(
        functools.partial(per_device, mesh.shape["tensor"], mesh.shape["replica"]),
        mesh=mesh,
        in_specs=(
            P(("groups", "replica"), "tensor"),
            P(None, "tensor"),
            P("tensor", None),
            P(("groups", "replica"), None, None, None),
            P(("groups", "replica"), None, None, None),
            P(("groups", "replica"), None, "tensor"),
            P(("groups", "replica"), None, "tensor"),
            P(("groups", "replica"), None, "tensor"),
            P(("groups", "replica"), None, "tensor"),
            P("groups"),
            P("groups"),
            P(("groups", "replica")),
        ),
        out_specs=P(("groups", "replica"), "tensor"),
        check_vma=False,
    )
```

```python
import functools
import math

import jax
import jax.numpy as jnp
from jax import lax
from jax.experimental import pallas as pl
from jax.experimental.pallas import tpu as pltpu
from jax.sharding import PartitionSpec as P

HEADS = 64
KVS = 8
ROW_BLOCK = 8
F32 = jnp.float32
BF16 = jnp.bfloat16


def loop(count, body, first=0):
    def step(k, carry):
        body(k)
        return carry

    if count > first:
        lax.fori_loop(first, count, step, 0)


def remote(src, dst, send_sem, recv_sem, device):
    return pltpu.make_async_remote_copy(
        src_ref=src,
        dst_ref=dst,
        send_sem=send_sem,
        recv_sem=recv_sem,
        device_id=device,
        device_id_type=pl.DeviceIdType.MESH,
    )


def block_kernel(
    tensor,
    replicas,
    hidden,
    w_query,
    output_weight,
    keys,
    values,
    query_down,
    query_up,
    output_down,
    output_up,
    ids,
    owners,
    lengths,
    out,
    h_buf,
    wq_buf,
    ow_buf,
    key_buf,
    value_buf,
    map_buf,
    acc,
    mixed,
    low_send,
    low_recv,
    pair_send,
    pair_recv,
    far_send,
    far_recv,
    h_local,
    wq_sem,
    ow_sem,
    kv_sem,
    map_local,
    map_send_sem,
    map_recv_sem,
    h_send_sem,
    h_recv_sem,
    fwd_send_sem,
    low_send_sem,
    low_recv_sem,
    pair_send_sem,
    pair_recv_sem,
    far_send_sem,
    far_recv_sem,
):
    rows, width = hidden.shape
    cols = w_query.shape[1]
    head_size = keys.shape[3]
    length = keys.shape[2]
    stored, rank, _ = query_down.shape
    adapters = stored * replicas
    lanes = low_send.shape[2]
    packed = lanes // rank
    inner = 2 if tensor % 2 == 0 else 1
    outer = tensor // inner
    me = lax.axis_index("tensor")
    rep = lax.axis_index("replica")
    o, i = me // inner, me % inner

    def at(k, j):
        return ((o + k) % outer) * inner + (i + j) % inner

    barrier = pltpu.get_barrier_semaphore()
    for k in range(1, tensor):
        pl.semaphore_signal(
            barrier, inc=1, device_id={"tensor": (me + k) % tensor}, device_id_type=pl.DeviceIdType.MESH
        )
    for k in range(1, replicas):
        pl.semaphore_signal(
            barrier, inc=1, device_id={"replica": (rep + k) % replicas}, device_id_type=pl.DeviceIdType.MESH
        )

    own_hidden = pltpu.make_async_copy(hidden, h_buf.at[me], h_local)
    own_hidden.start()
    maps = (query_down, query_up, output_down, output_up)
    own_slots = pl.ds(pl.multiple_of(rep * stored, stored), stored)
    own_maps = [
        pltpu.make_async_copy(maps[m], map_buf.at[m, own_slots], map_local.at[m]) for m in range(4)
    ]

    def shard(n):
        return ((o + outer - n % outer) % outer) * inner + (i + n // outer) % inner

    def target(n):
        return at((n + 1) % outer, inner - 1 - n // outer)

    def wq_copy(s):
        return pltpu.make_async_copy(
            w_query.at[pl.ds(pl.multiple_of(s * width, width), width), :], wq_buf.at[s], wq_sem.at[s]
        )

    def ow_copy(s):
        return pltpu.make_async_copy(
            output_weight.at[:, pl.ds(pl.multiple_of(s * width, width), width)], ow_buf.at[s], ow_sem.at[s]
        )

    own_maps[0].start()
    local_heads = cols // head_size
    group = HEADS // KVS
    kv_count = max(1, local_heads // group)
    first_kv = me * local_heads // group
    kv_copies = []
    for j in range(kv_count):
        kv_copies.append(pltpu.make_async_copy(keys.at[:, first_kv + j], key_buf.at[j], kv_sem.at[0, j]))
        kv_copies.append(pltpu.make_async_copy(values.at[:, first_kv + j], value_buf.at[j], kv_sem.at[1, j]))
    ahead = min(4, tensor)
    for n in range(ahead):
        wq_copy(shard(n)).start()

    pl.semaphore_wait(barrier, tensor - 1 + replicas - 1)
    own_hidden.wait()

    h_sends = []
    for k in range(1, outer):
        h_sends.append(
            remote(
                h_buf.at[me], h_buf.at[me], h_send_sem.at[k], h_recv_sem.at[me], {"tensor": at(k, 0)}
            )
        )
    if inner == 2:
        h_sends.append(
            remote(h_buf.at[me], h_buf.at[me], h_send_sem.at[0], h_recv_sem.at[me], {"tensor": at(0, 1)})
        )
    for copy in h_sends:
        copy.start()

    map_copies = []

    def send_map(m):
        for k in range(1, replicas):
            map_copies.append(
                remote(
                    maps[m],
                    map_buf.at[m, own_slots],
                    map_send_sem.at[m, k],
                    map_recv_sem.at[m, rep],
                    {"replica": (rep + k) % replicas},
                )
            )
            map_copies[-1].start()

    send_map(0)
    send_map(1)
    own_maps[1].start()
    for copy in kv_copies:
        copy.start()

    def wait_map(m):
        own_maps[m].wait()
        for k in range(1, replicas):
            other = (rep + k) % replicas
            block = map_buf.at[m, pl.ds(pl.multiple_of(other * stored, stored), stored)]
            remote(block, block, map_send_sem.at[m, k], map_recv_sem.at[m, other], {"replica": other}).wait_recv()

    def down_rows(line, first):
        size = line.shape[1]
        row = lax.broadcasted_iota(jnp.int32, (rows, size), 0) + first
        column = lax.broadcasted_iota(jnp.int32, (rows, size), 1)
        return jnp.sum(jnp.where(row == column, line.astype(F32), 0.0), axis=1, keepdims=True)

    own_ids = down_rows(ids[...], rep * rows)
    held = down_rows(lengths[...], 0)
    table = lax.broadcasted_iota(jnp.int32, (rows, owners.shape[1]), 1).astype(F32)
    slot = jnp.sum(jnp.where(own_ids == table, owners[...].astype(F32), 0.0), axis=1, keepdims=True)
    lane = lax.broadcasted_iota(jnp.int32, (rows, adapters * rank), 1) // rank
    pick = lane.astype(F32) == slot
    lower = lax.broadcasted_iota(jnp.int32, (rows // packed, lanes), 1) < rank

    def turned(x):
        return jnp.concatenate([x[:, rank:], x[:, :rank]], axis=1)

    def send_low(which, features):
        down = map_buf[2 * which].reshape(adapters * rank, width)
        part = lax.dot_general(features, down, (((1,), (1,)), ((), ())), preferred_element_type=F32)
        part = jnp.where(pick, part, 0.0)
        part = sum(part[:, c : c + lanes] for c in range(0, adapters * rank, lanes))
        if packed == 2:
            part = part + turned(part)
            part = jnp.where(lower, part[: rows // 2], part[rows // 2 :])
        low_send[which] = part
        copies = []
        for k in range(1, tensor):
            copies.append(
                remote(
                    low_send.at[which],
                    low_recv.at[which, me],
                    low_send_sem.at[which, k],
                    low_recv_sem.at[which, me],
                    {"tensor": (me + k) % tensor},
                )
            )
            copies[-1].start()
        return copies

    def adapter_delta(which):
        total = low_send[which]
        for k in range(1, tensor):
            s = (me + k) % tensor
            remote(
                low_send.at[which], low_recv.at[which, s], low_send_sem.at[which, k], low_recv_sem.at[which, s], {"tensor": s}
            ).wait_recv()
            total = total + low_recv[which, s]
        if packed == 2:
            other = turned(total)
            total = jnp.concatenate(
                [jnp.where(lower, total, other), jnp.where(lower, other, total)], axis=0
            )
        spread = jnp.concatenate([total] * (adapters * rank // lanes), axis=1)
        spread = jnp.where(pick, spread, 0.0).astype(BF16)
        up = map_buf[2 * which + 1].reshape(adapters * rank, width)
        return 0.5 * jnp.dot(spread, up, preferred_element_type=F32)

    def wait_hidden(s):
        remote(h_buf.at[s], h_buf.at[s], h_send_sem.at[0], h_recv_sem.at[s], {"tensor": at(0, 1)}).wait_recv()

    acc[...] = jnp.zeros_like(acc)

    def forward(n):
        s = shard(n)
        return remote(h_buf.at[s], h_buf.at[s], fwd_send_sem.at[n], h_recv_sem.at[s], {"tensor": at(0, 1)})

    def use_shard(n):
        following = shard(n + 1)

        @pl.when(n + 1 < tensor)
        def _():
            wait_hidden(following)

        if inner == 2:

            @pl.when(n + 1 < outer)
            def _():
                forward(n + 1).start()

        @pl.when(n + ahead < tensor)
        def _():
            wq_copy(shard(n + ahead)).start()

        ow_copy(target(n)).start()
        s = shard(n)
        wq_copy(s).wait()
        acc[...] += jnp.dot(h_buf[s], wq_buf[s], preferred_element_type=F32)

    first, second = tensor * 3 // 8, tensor * 7 // 8
    loop(first, use_shard)
    wait_map(0)
    low_copies = send_low(0, h_buf[me])
    loop(second, use_shard, first)
    wait_map(1)
    acc[...] += adapter_delta(0)
    loop(tensor, use_shard, second)
    for m in range(2, 4):
        send_map(m)
        own_maps[m].start()
    query = acc[...]

    for copy in kv_copies:
        copy.wait()
    per_kv = local_heads // kv_count
    shape = (per_kv * ROW_BLOCK, ROW_BLOCK * length)
    row = lax.broadcasted_iota(jnp.int32, shape, 0) % ROW_BLOCK
    column = lax.broadcasted_iota(jnp.int32, shape, 1)
    position = (column - row * length).astype(F32)
    for j in range(kv_count):
        for b in range(0, rows, ROW_BLOCK):
            heads = [
                query[b : b + ROW_BLOCK, h * head_size : (h + 1) * head_size]
                for h in range(j * per_kv, (j + 1) * per_kv)
            ]
            q = jnp.concatenate(heads, axis=0).astype(BF16)
            key = key_buf[j, b : b + ROW_BLOCK].reshape(ROW_BLOCK * length, head_size)
            value = value_buf[j, b : b + ROW_BLOCK].reshape(ROW_BLOCK * length, head_size)
            live = jnp.concatenate([held[b : b + ROW_BLOCK]] * per_kv, axis=0)
            scores = lax.dot_general(q, key, (((1,), (1,)), ((), ())), preferred_element_type=F32)
            scores = scores * (1.0 / math.sqrt(head_size))
            scores = jnp.where((position >= 0) & (position < live), scores, -1e30)
            top = jnp.max(scores, axis=1, keepdims=True)
            weights = jnp.exp(scores - top)
            probs = (weights / jnp.sum(weights, axis=1, keepdims=True)).astype(BF16)
            result = jnp.dot(probs, value, preferred_element_type=F32)
            for n in range(per_kv):
                h = j * per_kv + n
                mixed[b : b + ROW_BLOCK, h * head_size : (h + 1) * head_size] = result[
                    n * ROW_BLOCK : (n + 1) * ROW_BLOCK
                ]

    features = mixed[...].astype(BF16)
    def pair_copy(k):
        d = (o + k) % outer
        return remote(
            pair_send.at[k], pair_recv.at[d], pair_send_sem.at[k], pair_recv_sem.at[d], {"tensor": at(0, 1)}
        )

    def far_copy(k):
        return remote(far_send.at[k], far_recv.at[o], far_send_sem.at[k], far_recv_sem.at[o], {"tensor": at(k, 0)})

    def product(s):
        ow_copy(s).wait()
        return jnp.dot(features, ow_buf[s], preferred_element_type=F32)

    def to_pair(n):
        k = (n + 1) % outer
        pair_send[k] = product(at(k, 1)).astype(BF16)
        pair_copy(k).start()

    early = outer // 2 if inner == 2 else 0
    loop(early, to_pair)
    wait_map(2)
    low_copies += send_low(1, features)
    if inner == 2:
        loop(outer, to_pair, early)

    def own_sum(k):
        total = product(at(k, 0))
        if inner == 2:
            pair_copy(k).wait_recv()
            total = total + pair_recv[(o + k) % outer].astype(F32)
        return total

    def to_far(k):
        far_send[k] = own_sum(k).astype(BF16)
        far_copy(k).start()

    loop(outer, to_far, 1)
    wait_map(3)
    total = adapter_delta(1)
    total = total + own_sum(0)
    for k in range(1, outer):
        s = (o + k) % outer
        remote(far_send.at[k], far_recv.at[s], far_send_sem.at[k], far_recv_sem.at[s], {"tensor": at(k, 0)}).wait_recv()
        total = total + far_recv[s].astype(F32)
    out[...] = total.astype(BF16)

    for copy in h_sends + map_copies + low_copies:
        copy.wait_send()
    for k in range(outer):
        if k > 0:
            far_copy(k).wait_send()
        if inner == 2:
            pair_copy(k).wait_send()
            if k > 0:
                forward(k).wait_send()


def per_device(tensor, replicas, *args):
    (
        hidden,
        w_query,
        output_weight,
        keys,
        values,
        query_down,
        query_up,
        output_down,
        output_up,
        adapter_ids,
        owner_map,
        kv_lengths,
    ) = args
    rows, width = hidden.shape
    cols = w_query.shape[1]
    stored, rank, _ = query_down.shape
    length, head_size = keys.shape[2:]
    kv_count = max(1, cols // head_size // (HEADS // KVS))
    inner = 2 if tensor % 2 == 0 else 1
    outer = tensor // inner
    lanes = max(128, rank)
    dma = pltpu.SemaphoreType.DMA
    any_spec = pl.BlockSpec(memory_space=pl.ANY)
    vmem_spec = pl.BlockSpec(memory_space=pltpu.VMEM)
    return pl.pallas_call(
        functools.partial(block_kernel, tensor, replicas),
        out_shape=pltpu.VMEM((rows, width), BF16),
        in_specs=[any_spec] * 9 + [vmem_spec] * 3,
        out_specs=vmem_spec,
        scratch_shapes=[
            pltpu.VMEM((tensor, rows, width), BF16),
            pltpu.VMEM((tensor, width, cols), BF16),
            pltpu.VMEM((tensor, cols, width), BF16),
            pltpu.VMEM((kv_count, rows, length, head_size), BF16),
            pltpu.VMEM((kv_count, rows, length, head_size), BF16),
            pltpu.VMEM((4, replicas * stored, rank, width), BF16),
            pltpu.VMEM((rows, cols), F32),
            pltpu.VMEM((rows, cols), F32),
            pltpu.VMEM((2, rows * rank // lanes, lanes), F32),
            pltpu.VMEM((2, tensor, rows * rank // lanes, lanes), F32),
            pltpu.VMEM((outer, rows, width), BF16),
            pltpu.VMEM((outer, rows, width), BF16),
            pltpu.VMEM((outer, rows, width), BF16),
            pltpu.VMEM((outer, rows, width), BF16),
            dma,
            dma((tensor,)),
            dma((tensor,)),
            dma((2, kv_count)),
            dma((4,)),
            dma((4, replicas)),
            dma((4, replicas)),
            dma((outer,)),
            dma((tensor,)),
            dma((outer,)),
            dma((2, tensor)),
            dma((2, tensor)),
            dma((outer,)),
            dma((outer,)),
            dma((outer,)),
            dma((outer,)),
        ],
        compiler_params=pltpu.CompilerParams(
            collective_id=0, has_side_effects=True, vmem_limit_bytes=58 * 1024 * 1024
        ),
    )(
        hidden,
        w_query,
        output_weight,
        keys,
        values,
        query_down,
        query_up,
        output_down,
        output_up,
        adapter_ids.reshape(1, -1),
        owner_map.reshape(1, -1),
        kv_lengths.reshape(1, -1),
    )


def solution(mesh):
    return jax.shard_map(
        functools.partial(per_device, mesh.shape["tensor"], mesh.shape["replica"]),
        mesh=mesh,
        in_specs=(
            P(("groups", "replica"), "tensor"),
            P(None, "tensor"),
            P("tensor", None),
            P(("groups", "replica"), None, None, None),
            P(("groups", "replica"), None, None, None),
            P(("groups", "replica"), None, "tensor"),
            P(("groups", "replica"), None, "tensor"),
            P(("groups", "replica"), None, "tensor"),
            P(("groups", "replica"), None, "tensor"),
            P("groups"),
            P("groups"),
            P(("groups", "replica")),
        ),
        out_specs=P(("groups", "replica"), "tensor"),
        check_vma=False,
    )
```

```python
import functools
import math

import jax
import jax.numpy as jnp
from jax import lax
from jax.experimental import pallas as pl
from jax.experimental.pallas import tpu as pltpu
from jax.sharding import PartitionSpec as P

HEADS = 64
KVS = 8
ROW_BLOCK = 8
F32 = jnp.float32
BF16 = jnp.bfloat16


def loop(count, body, first=0):
    def step(k, carry):
        body(k)
        return carry

    if count > first:
        lax.fori_loop(first, count, step, 0)


def remote(src, dst, send_sem, recv_sem, device):
    return pltpu.make_async_remote_copy(
        src_ref=src,
        dst_ref=dst,
        send_sem=send_sem,
        recv_sem=recv_sem,
        device_id=device,
        device_id_type=pl.DeviceIdType.MESH,
    )


def block_kernel(
    tensor,
    replicas,
    hidden,
    w_query,
    output_weight,
    keys,
    values,
    query_down,
    query_up,
    output_down,
    output_up,
    ids,
    owners,
    lengths,
    out,
    h_buf,
    wq_buf,
    ow_buf,
    key_buf,
    value_buf,
    map_buf,
    acc,
    mixed,
    low_send,
    low_recv,
    pair_send,
    pair_recv,
    far_send,
    far_recv,
    h_local,
    wq_sem,
    ow_sem,
    kv_sem,
    map_local,
    map_send_sem,
    map_recv_sem,
    h_send_sem,
    h_recv_sem,
    fwd_send_sem,
    low_send_sem,
    low_recv_sem,
    pair_send_sem,
    pair_recv_sem,
    far_send_sem,
    far_recv_sem,
):
    rows, width = hidden.shape
    cols = w_query.shape[1]
    head_size = keys.shape[3]
    length = keys.shape[2]
    stored, rank, _ = query_down.shape
    adapters = stored * replicas
    lanes = low_send.shape[2]
    packed = lanes // rank
    inner = 2 if tensor % 2 == 0 else 1
    outer = tensor // inner
    me = lax.axis_index("tensor")
    rep = lax.axis_index("replica")
    o, i = me // inner, me % inner

    def at(k, j):
        return ((o + k) % outer) * inner + (i + j) % inner

    barrier = pltpu.get_barrier_semaphore()
    for k in range(1, tensor):
        pl.semaphore_signal(
            barrier, inc=1, device_id={"tensor": (me + k) % tensor}, device_id_type=pl.DeviceIdType.MESH
        )
    for k in range(1, replicas):
        pl.semaphore_signal(
            barrier, inc=1, device_id={"replica": (rep + k) % replicas}, device_id_type=pl.DeviceIdType.MESH
        )

    own_hidden = pltpu.make_async_copy(hidden, h_buf.at[me], h_local)
    own_hidden.start()
    maps = (query_down, query_up, output_down, output_up)
    own_slots = pl.ds(pl.multiple_of(rep * stored, stored), stored)
    own_maps = [
        pltpu.make_async_copy(maps[m], map_buf.at[m, own_slots], map_local.at[m]) for m in range(4)
    ]

    def shard(n):
        return ((o + outer - n % outer) % outer) * inner + (i + n // outer) % inner

    def target(n):
        return at((n + 1) % outer, inner - 1 - n // outer)

    def wq_copy(s):
        return pltpu.make_async_copy(
            w_query.at[pl.ds(pl.multiple_of(s * width, width), width), :], wq_buf.at[s], wq_sem.at[s]
        )

    def ow_copy(s):
        return pltpu.make_async_copy(
            output_weight.at[:, pl.ds(pl.multiple_of(s * width, width), width)], ow_buf.at[s], ow_sem.at[s]
        )

    own_maps[0].start()
    local_heads = cols // head_size
    group = HEADS // KVS
    kv_count = max(1, local_heads // group)
    first_kv = me * local_heads // group
    kv_copies = []
    for j in range(kv_count):
        kv_copies.append(pltpu.make_async_copy(keys.at[:, first_kv + j], key_buf.at[j], kv_sem.at[0, j]))
        kv_copies.append(pltpu.make_async_copy(values.at[:, first_kv + j], value_buf.at[j], kv_sem.at[1, j]))
    ahead = min(4, tensor)
    for n in range(ahead):
        wq_copy(shard(n)).start()

    pl.semaphore_wait(barrier, tensor - 1 + replicas - 1)
    own_hidden.wait()

    h_sends = []
    if inner == 2:
        h_sends.append(
            remote(h_buf.at[me], h_buf.at[me], h_send_sem.at[0], h_recv_sem.at[me], {"tensor": at(0, 1)})
        )
    for k in range(1, outer):
        h_sends.append(
            remote(
                h_buf.at[me], h_buf.at[me], h_send_sem.at[k], h_recv_sem.at[me], {"tensor": at(k, 0)}
            )
        )
    for copy in h_sends:
        copy.start()

    map_copies = []

    def send_map(m):
        for k in range(1, replicas):
            map_copies.append(
                remote(
                    maps[m],
                    map_buf.at[m, own_slots],
                    map_send_sem.at[m, k],
                    map_recv_sem.at[m, rep],
                    {"replica": (rep + k) % replicas},
                )
            )
            map_copies[-1].start()

    send_map(0)
    own_maps[1].start()
    for copy in kv_copies:
        copy.start()

    def wait_map(m):
        own_maps[m].wait()
        for k in range(1, replicas):
            other = (rep + k) % replicas
            block = map_buf.at[m, pl.ds(pl.multiple_of(other * stored, stored), stored)]
            remote(block, block, map_send_sem.at[m, k], map_recv_sem.at[m, other], {"replica": other}).wait_recv()

    def down_rows(line, first):
        size = line.shape[1]
        row = lax.broadcasted_iota(jnp.int32, (rows, size), 0) + first
        column = lax.broadcasted_iota(jnp.int32, (rows, size), 1)
        return jnp.sum(jnp.where(row == column, line.astype(F32), 0.0), axis=1, keepdims=True)

    own_ids = down_rows(ids[...], rep * rows)
    held = down_rows(lengths[...], 0)
    table = lax.broadcasted_iota(jnp.int32, (rows, owners.shape[1]), 1).astype(F32)
    slot = jnp.sum(jnp.where(own_ids == table, owners[...].astype(F32), 0.0), axis=1, keepdims=True)
    lane = lax.broadcasted_iota(jnp.int32, (rows, adapters * rank), 1) // rank
    pick = lane.astype(F32) == slot
    lower = lax.broadcasted_iota(jnp.int32, (rows // packed, lanes), 1) < rank

    def turned(x):
        return jnp.concatenate([x[:, rank:], x[:, :rank]], axis=1)

    def send_low(which, features):
        down = map_buf[2 * which].reshape(adapters * rank, width)
        part = lax.dot_general(features, down, (((1,), (1,)), ((), ())), preferred_element_type=F32)
        part = jnp.where(pick, part, 0.0)
        part = sum(part[:, c : c + lanes] for c in range(0, adapters * rank, lanes))
        if packed == 2:
            part = part + turned(part)
            part = jnp.where(lower, part[: rows // 2], part[rows // 2 :])
        low_send[which] = part
        copies = []
        for k in range(1, tensor):
            copies.append(
                remote(
                    low_send.at[which],
                    low_recv.at[which, me],
                    low_send_sem.at[which, k],
                    low_recv_sem.at[which, me],
                    {"tensor": (me + k) % tensor},
                )
            )
            copies[-1].start()
        return copies

    def adapter_delta(which):
        total = low_send[which]
        for k in range(1, tensor):
            s = (me + k) % tensor
            remote(
                low_send.at[which], low_recv.at[which, s], low_send_sem.at[which, k], low_recv_sem.at[which, s], {"tensor": s}
            ).wait_recv()
            total = total + low_recv[which, s]
        if packed == 2:
            other = turned(total)
            total = jnp.concatenate(
                [jnp.where(lower, total, other), jnp.where(lower, other, total)], axis=0
            )
        spread = jnp.concatenate([total] * (adapters * rank // lanes), axis=1)
        spread = jnp.where(pick, spread, 0.0).astype(BF16)
        up = map_buf[2 * which + 1].reshape(adapters * rank, width)
        return 0.5 * jnp.dot(spread, up, preferred_element_type=F32)

    def wait_hidden(s):
        remote(h_buf.at[s], h_buf.at[s], h_send_sem.at[0], h_recv_sem.at[s], {"tensor": at(0, 1)}).wait_recv()

    acc[...] = jnp.zeros_like(acc)

    def forward(n):
        s = shard(n)
        return remote(h_buf.at[s], h_buf.at[s], fwd_send_sem.at[n], h_recv_sem.at[s], {"tensor": at(0, 1)})

    def use_shard(n):
        following = shard(n + 1)

        @pl.when(n + 1 < tensor)
        def _():
            wait_hidden(following)

        if inner == 2:

            @pl.when(n + 1 < outer)
            def _():
                forward(n + 1).start()

        @pl.when(n + ahead < tensor)
        def _():
            wq_copy(shard(n + ahead)).start()

        ow_copy(target(n)).start()
        s = shard(n)
        wq_copy(s).wait()
        acc[...] += jnp.dot(h_buf[s], wq_buf[s], preferred_element_type=F32)

    first, second = tensor * 3 // 8, tensor * 7 // 8
    loop(first, use_shard)
    send_map(1)
    wait_map(0)
    low_copies = send_low(0, h_buf[me])
    loop(second, use_shard, first)
    wait_map(1)
    acc[...] += adapter_delta(0)
    loop(tensor, use_shard, second)
    for m in range(2, 4):
        send_map(m)
        own_maps[m].start()
    query = acc[...]

    for copy in kv_copies:
        copy.wait()
    per_kv = local_heads // kv_count
    shape = (per_kv * ROW_BLOCK, ROW_BLOCK * length)
    row = lax.broadcasted_iota(jnp.int32, shape, 0) % ROW_BLOCK
    column = lax.broadcasted_iota(jnp.int32, shape, 1)
    position = (column - row * length).astype(F32)
    for j in range(kv_count):
        for b in range(0, rows, ROW_BLOCK):
            heads = [
                query[b : b + ROW_BLOCK, h * head_size : (h + 1) * head_size]
                for h in range(j * per_kv, (j + 1) * per_kv)
            ]
            q = jnp.concatenate(heads, axis=0).astype(BF16)
            key = key_buf[j, b : b + ROW_BLOCK].reshape(ROW_BLOCK * length, head_size)
            value = value_buf[j, b : b + ROW_BLOCK].reshape(ROW_BLOCK * length, head_size)
            live = jnp.concatenate([held[b : b + ROW_BLOCK]] * per_kv, axis=0)
            scores = lax.dot_general(q, key, (((1,), (1,)), ((), ())), preferred_element_type=F32)
            scores = scores * (1.0 / math.sqrt(head_size))
            scores = jnp.where((position >= 0) & (position < live), scores, -1e30)
            top = jnp.max(scores, axis=1, keepdims=True)
            weights = jnp.exp(scores - top)
            probs = (weights / jnp.sum(weights, axis=1, keepdims=True)).astype(BF16)
            result = jnp.dot(probs, value, preferred_element_type=F32)
            for n in range(per_kv):
                h = j * per_kv + n
                mixed[b : b + ROW_BLOCK, h * head_size : (h + 1) * head_size] = result[
                    n * ROW_BLOCK : (n + 1) * ROW_BLOCK
                ]

    features = mixed[...].astype(BF16)
    def pair_copy(k):
        d = (o + k) % outer
        return remote(
            pair_send.at[k], pair_recv.at[d], pair_send_sem.at[k], pair_recv_sem.at[d], {"tensor": at(0, 1)}
        )

    def far_copy(k):
        return remote(far_send.at[k], far_recv.at[o], far_send_sem.at[k], far_recv_sem.at[o], {"tensor": at(k, 0)})

    def product(s):
        ow_copy(s).wait()
        return jnp.dot(features, ow_buf[s], preferred_element_type=F32)

    def to_pair(n):
        k = (n + 1) % outer
        pair_send[k] = product(at(k, 1)).astype(BF16)
        pair_copy(k).start()

    def own_sum(k):
        total = product(at(k, 0))
        if inner == 2:
            pair_copy(k).wait_recv()
            total = total + pair_recv[(o + k) % outer].astype(F32)
        return total

    def to_far(k):
        far_send[k] = own_sum(k).astype(BF16)
        far_copy(k).start()

    early = min(2, outer) if inner == 2 else 0
    loop(early, to_pair)
    wait_map(2)
    low_copies += send_low(1, features)

    def both(n):
        to_far(n - early + 1)
        to_pair(n)

    if inner == 2:
        loop(outer, both, early)
        loop(outer, to_far, outer - early + 1)
    else:
        loop(outer, to_far, 1)
    wait_map(3)
    total = adapter_delta(1)
    total = total + own_sum(0)
    for k in range(1, outer):
        s = (o + k) % outer
        remote(far_send.at[k], far_recv.at[s], far_send_sem.at[k], far_recv_sem.at[s], {"tensor": at(k, 0)}).wait_recv()
        total = total + far_recv[s].astype(F32)
    out[...] = total.astype(BF16)

    for copy in h_sends + map_copies + low_copies:
        copy.wait_send()
    for k in range(outer):
        if k > 0:
            far_copy(k).wait_send()
        if inner == 2:
            pair_copy(k).wait_send()
            if k > 0:
                forward(k).wait_send()


def per_device(tensor, replicas, *args):
    (
        hidden,
        w_query,
        output_weight,
        keys,
        values,
        query_down,
        query_up,
        output_down,
        output_up,
        adapter_ids,
        owner_map,
        kv_lengths,
    ) = args
    rows, width = hidden.shape
    cols = w_query.shape[1]
    stored, rank, _ = query_down.shape
    length, head_size = keys.shape[2:]
    kv_count = max(1, cols // head_size // (HEADS // KVS))
    inner = 2 if tensor % 2 == 0 else 1
    outer = tensor // inner
    lanes = max(128, rank)
    dma = pltpu.SemaphoreType.DMA
    any_spec = pl.BlockSpec(memory_space=pl.ANY)
    vmem_spec = pl.BlockSpec(memory_space=pltpu.VMEM)
    return pl.pallas_call(
        functools.partial(block_kernel, tensor, replicas),
        out_shape=pltpu.VMEM((rows, width), BF16),
        in_specs=[any_spec] * 9 + [vmem_spec] * 3,
        out_specs=vmem_spec,
        scratch_shapes=[
            pltpu.VMEM((tensor, rows, width), BF16),
            pltpu.VMEM((tensor, width, cols), BF16),
            pltpu.VMEM((tensor, cols, width), BF16),
            pltpu.VMEM((kv_count, rows, length, head_size), BF16),
            pltpu.VMEM((kv_count, rows, length, head_size), BF16),
            pltpu.VMEM((4, replicas * stored, rank, width), BF16),
            pltpu.VMEM((rows, cols), F32),
            pltpu.VMEM((rows, cols), F32),
            pltpu.VMEM((2, rows * rank // lanes, lanes), F32),
            pltpu.VMEM((2, tensor, rows * rank // lanes, lanes), F32),
            pltpu.VMEM((outer, rows, width), BF16),
            pltpu.VMEM((outer, rows, width), BF16),
            pltpu.VMEM((outer, rows, width), BF16),
            pltpu.VMEM((outer, rows, width), BF16),
            dma,
            dma((tensor,)),
            dma((tensor,)),
            dma((2, kv_count)),
            dma((4,)),
            dma((4, replicas)),
            dma((4, replicas)),
            dma((outer,)),
            dma((tensor,)),
            dma((outer,)),
            dma((2, tensor)),
            dma((2, tensor)),
            dma((outer,)),
            dma((outer,)),
            dma((outer,)),
            dma((outer,)),
        ],
        compiler_params=pltpu.CompilerParams(
            collective_id=0, has_side_effects=True, vmem_limit_bytes=58 * 1024 * 1024
        ),
    )(
        hidden,
        w_query,
        output_weight,
        keys,
        values,
        query_down,
        query_up,
        output_down,
        output_up,
        adapter_ids.reshape(1, -1),
        owner_map.reshape(1, -1),
        kv_lengths.reshape(1, -1),
    )


def solution(mesh):
    return jax.shard_map(
        functools.partial(per_device, mesh.shape["tensor"], mesh.shape["replica"]),
        mesh=mesh,
        in_specs=(
            P(("groups", "replica"), "tensor"),
            P(None, "tensor"),
            P("tensor", None),
            P(("groups", "replica"), None, None, None),
            P(("groups", "replica"), None, None, None),
            P(("groups", "replica"), None, "tensor"),
            P(("groups", "replica"), None, "tensor"),
            P(("groups", "replica"), None, "tensor"),
            P(("groups", "replica"), None, "tensor"),
            P("groups"),
            P("groups"),
            P(("groups", "replica")),
        ),
        out_specs=P(("groups", "replica"), "tensor"),
        check_vma=False,
    )
```

```python
import functools
import math

import jax
import jax.numpy as jnp
from jax import lax
from jax.experimental import pallas as pl
from jax.experimental.pallas import tpu as pltpu
from jax.sharding import PartitionSpec as P

HEADS = 64
KVS = 8
ROW_BLOCK = 8
F32 = jnp.float32
BF16 = jnp.bfloat16


def loop(count, body, first=0):
    def step(k, carry):
        body(k)
        return carry

    if count > first:
        lax.fori_loop(first, count, step, 0)


def remote(src, dst, send_sem, recv_sem, device):
    return pltpu.make_async_remote_copy(
        src_ref=src,
        dst_ref=dst,
        send_sem=send_sem,
        recv_sem=recv_sem,
        device_id=device,
        device_id_type=pl.DeviceIdType.MESH,
    )


def block_kernel(
    tensor,
    replicas,
    hidden,
    w_query,
    output_weight,
    keys,
    values,
    query_down,
    query_up,
    output_down,
    output_up,
    ids,
    owners,
    lengths,
    out,
    h_buf,
    wq_buf,
    ow_buf,
    key_buf,
    value_buf,
    map_buf,
    acc,
    mixed,
    low_send,
    low_recv,
    pair_send,
    pair_recv,
    far_send,
    far_recv,
    h_local,
    wq_sem,
    ow_sem,
    kv_sem,
    map_local,
    map_send_sem,
    map_recv_sem,
    h_send_sem,
    h_recv_sem,
    fwd_send_sem,
    low_send_sem,
    low_recv_sem,
    pair_send_sem,
    pair_recv_sem,
    far_send_sem,
    far_recv_sem,
):
    rows, width = hidden.shape
    cols = w_query.shape[1]
    head_size = keys.shape[3]
    length = keys.shape[2]
    stored, rank, _ = query_down.shape
    adapters = stored * replicas
    lanes = low_send.shape[2]
    packed = lanes // rank
    inner = 2 if tensor % 2 == 0 else 1
    outer = tensor // inner
    me = lax.axis_index("tensor")
    rep = lax.axis_index("replica")
    o, i = me // inner, me % inner

    def at(k, j):
        return ((o + k) % outer) * inner + (i + j) % inner

    barrier = pltpu.get_barrier_semaphore()
    for k in range(1, tensor):
        pl.semaphore_signal(
            barrier, inc=1, device_id={"tensor": (me + k) % tensor}, device_id_type=pl.DeviceIdType.MESH
        )
    for k in range(1, replicas):
        pl.semaphore_signal(
            barrier, inc=1, device_id={"replica": (rep + k) % replicas}, device_id_type=pl.DeviceIdType.MESH
        )

    own_hidden = pltpu.make_async_copy(hidden, h_buf.at[me], h_local)
    own_hidden.start()
    maps = (query_down, query_up, output_down, output_up)
    own_slots = pl.ds(pl.multiple_of(rep * stored, stored), stored)
    own_maps = [
        pltpu.make_async_copy(maps[m], map_buf.at[m, own_slots], map_local.at[m]) for m in range(4)
    ]

    def shard(n):
        return ((o + outer - n % outer) % outer) * inner + (i + n // outer) % inner

    def target(n):
        return at((n + 1) % outer, inner - 1 - n // outer)

    def wq_copy(s):
        return pltpu.make_async_copy(
            w_query.at[pl.ds(pl.multiple_of(s * width, width), width), :], wq_buf.at[s], wq_sem.at[s]
        )

    def ow_copy(s):
        return pltpu.make_async_copy(
            output_weight.at[:, pl.ds(pl.multiple_of(s * width, width), width)], ow_buf.at[s], ow_sem.at[s]
        )

    own_maps[0].start()
    local_heads = cols // head_size
    group = HEADS // KVS
    kv_count = max(1, local_heads // group)
    first_kv = me * local_heads // group
    kv_copies = []
    for j in range(kv_count):
        kv_copies.append(pltpu.make_async_copy(keys.at[:, first_kv + j], key_buf.at[j], kv_sem.at[0, j]))
        kv_copies.append(pltpu.make_async_copy(values.at[:, first_kv + j], value_buf.at[j], kv_sem.at[1, j]))
    ahead = tensor // 2
    for n in range(ahead):
        wq_copy(shard(n)).start()

    pl.semaphore_wait(barrier, tensor - 1 + replicas - 1)
    own_hidden.wait()

    h_sends = []
    if inner == 2:
        h_sends.append(
            remote(h_buf.at[me], h_buf.at[me], h_send_sem.at[0], h_recv_sem.at[me], {"tensor": at(0, 1)})
        )
    for k in range(1, outer):
        h_sends.append(
            remote(
                h_buf.at[me], h_buf.at[me], h_send_sem.at[k], h_recv_sem.at[me], {"tensor": at(k, 0)}
            )
        )
    for copy in h_sends:
        copy.start()

    map_copies = []

    def send_map(m):
        for k in range(1, replicas):
            map_copies.append(
                remote(
                    maps[m],
                    map_buf.at[m, own_slots],
                    map_send_sem.at[m, k],
                    map_recv_sem.at[m, rep],
                    {"replica": (rep + k) % replicas},
                )
            )
            map_copies[-1].start()

    send_map(0)
    own_maps[1].start()
    for copy in kv_copies:
        copy.start()

    def wait_map(m):
        own_maps[m].wait()
        for k in range(1, replicas):
            other = (rep + k) % replicas
            block = map_buf.at[m, pl.ds(pl.multiple_of(other * stored, stored), stored)]
            remote(block, block, map_send_sem.at[m, k], map_recv_sem.at[m, other], {"replica": other}).wait_recv()

    def down_rows(line, first):
        size = line.shape[1]
        row = lax.broadcasted_iota(jnp.int32, (rows, size), 0) + first
        column = lax.broadcasted_iota(jnp.int32, (rows, size), 1)
        return jnp.sum(jnp.where(row == column, line.astype(F32), 0.0), axis=1, keepdims=True)

    own_ids = down_rows(ids[...], rep * rows)
    held = down_rows(lengths[...], 0)
    table = lax.broadcasted_iota(jnp.int32, (rows, owners.shape[1]), 1).astype(F32)
    slot = jnp.sum(jnp.where(own_ids == table, owners[...].astype(F32), 0.0), axis=1, keepdims=True)
    lane = lax.broadcasted_iota(jnp.int32, (rows, adapters * rank), 1) // rank
    pick = lane.astype(F32) == slot
    lower = lax.broadcasted_iota(jnp.int32, (rows // packed, lanes), 1) < rank

    def turned(x):
        return jnp.concatenate([x[:, rank:], x[:, :rank]], axis=1)

    def send_low(which, features):
        down = map_buf[2 * which].reshape(adapters * rank, width)
        part = lax.dot_general(features, down, (((1,), (1,)), ((), ())), preferred_element_type=F32)
        part = jnp.where(pick, part, 0.0)
        part = sum(part[:, c : c + lanes] for c in range(0, adapters * rank, lanes))
        if packed == 2:
            part = part + turned(part)
            part = jnp.where(lower, part[: rows // 2], part[rows // 2 :])
        low_send[which] = part
        copies = []
        for k in range(1, tensor):
            copies.append(
                remote(
                    low_send.at[which],
                    low_recv.at[which, me],
                    low_send_sem.at[which, k],
                    low_recv_sem.at[which, me],
                    {"tensor": (me + k) % tensor},
                )
            )
            copies[-1].start()
        return copies

    def adapter_delta(which):
        total = low_send[which]
        for k in range(1, tensor):
            s = (me + k) % tensor
            remote(
                low_send.at[which], low_recv.at[which, s], low_send_sem.at[which, k], low_recv_sem.at[which, s], {"tensor": s}
            ).wait_recv()
            total = total + low_recv[which, s]
        if packed == 2:
            other = turned(total)
            total = jnp.concatenate(
                [jnp.where(lower, total, other), jnp.where(lower, other, total)], axis=0
            )
        spread = jnp.concatenate([total] * (adapters * rank // lanes), axis=1)
        spread = jnp.where(pick, spread, 0.0).astype(BF16)
        up = map_buf[2 * which + 1].reshape(adapters * rank, width)
        return 0.5 * jnp.dot(spread, up, preferred_element_type=F32)

    def wait_hidden(s):
        remote(h_buf.at[s], h_buf.at[s], h_send_sem.at[0], h_recv_sem.at[s], {"tensor": at(0, 1)}).wait_recv()

    acc[...] = jnp.zeros_like(acc)

    def forward(n):
        s = shard(n)
        return remote(h_buf.at[s], h_buf.at[s], fwd_send_sem.at[n], h_recv_sem.at[s], {"tensor": at(0, 1)})

    def use_shard(n):
        following = shard(n + 1)

        @pl.when(n + 1 < tensor)
        def _():
            wait_hidden(following)

        if inner == 2:

            @pl.when(n + 1 < outer)
            def _():
                forward(n + 1).start()

        @pl.when(n + ahead < tensor)
        def _():
            wq_copy(shard(n + ahead)).start()

        @pl.when(n >= tensor // 2)
        def _():
            for c in range(2):
                ow_copy(target(2 * n - tensor + c)).start()

        s = shard(n)
        wq_copy(s).wait()
        acc[...] += jnp.dot(h_buf[s], wq_buf[s], preferred_element_type=F32)

    first, second = tensor * 3 // 8, tensor * 7 // 8
    loop(first, use_shard)
    send_map(1)
    wait_map(0)
    low_copies = send_low(0, h_buf[me])
    loop(second, use_shard, first)
    wait_map(1)
    acc[...] += adapter_delta(0)
    loop(tensor, use_shard, second)
    for m in range(2, 4):
        send_map(m)
        own_maps[m].start()
    query = acc[...]

    for copy in kv_copies:
        copy.wait()
    per_kv = local_heads // kv_count
    shape = (per_kv * ROW_BLOCK, ROW_BLOCK * length)
    row = lax.broadcasted_iota(jnp.int32, shape, 0) % ROW_BLOCK
    column = lax.broadcasted_iota(jnp.int32, shape, 1)
    position = (column - row * length).astype(F32)
    for j in range(kv_count):
        for b in range(0, rows, ROW_BLOCK):
            heads = [
                query[b : b + ROW_BLOCK, h * head_size : (h + 1) * head_size]
                for h in range(j * per_kv, (j + 1) * per_kv)
            ]
            q = jnp.concatenate(heads, axis=0).astype(BF16)
            key = key_buf[j, b : b + ROW_BLOCK].reshape(ROW_BLOCK * length, head_size)
            value = value_buf[j, b : b + ROW_BLOCK].reshape(ROW_BLOCK * length, head_size)
            live = jnp.concatenate([held[b : b + ROW_BLOCK]] * per_kv, axis=0)
            scores = lax.dot_general(q, key, (((1,), (1,)), ((), ())), preferred_element_type=F32)
            scores = scores * (1.0 / math.sqrt(head_size))
            scores = jnp.where((position >= 0) & (position < live), scores, -1e30)
            top = jnp.max(scores, axis=1, keepdims=True)
            weights = jnp.exp(scores - top)
            probs = (weights / jnp.sum(weights, axis=1, keepdims=True)).astype(BF16)
            result = jnp.dot(probs, value, preferred_element_type=F32)
            for n in range(per_kv):
                h = j * per_kv + n
                mixed[b : b + ROW_BLOCK, h * head_size : (h + 1) * head_size] = result[
                    n * ROW_BLOCK : (n + 1) * ROW_BLOCK
                ]

    features = mixed[...].astype(BF16)
    def pair_copy(k):
        d = (o + k) % outer
        return remote(
            pair_send.at[k], pair_recv.at[d], pair_send_sem.at[k], pair_recv_sem.at[d], {"tensor": at(0, 1)}
        )

    def far_copy(k):
        return remote(far_send.at[k], far_recv.at[o], far_send_sem.at[k], far_recv_sem.at[o], {"tensor": at(k, 0)})

    def product(s):
        ow_copy(s).wait()
        return jnp.dot(features, ow_buf[s], preferred_element_type=F32)

    def to_pair(n):
        k = (n + 1) % outer
        pair_send[k] = product(at(k, 1)).astype(BF16)
        pair_copy(k).start()

    def own_sum(k):
        total = product(at(k, 0))
        if inner == 2:
            pair_copy(k).wait_recv()
            total = total + pair_recv[(o + k) % outer].astype(F32)
        return total

    def to_far(k):
        far_send[k] = own_sum(k).astype(BF16)
        far_copy(k).start()

    early = min(2, outer) if inner == 2 else 0
    loop(early, to_pair)
    wait_map(2)
    low_copies += send_low(1, features)

    def both(n):
        to_far(n - early + 1)
        to_pair(n)

    if inner == 2:
        loop(outer, both, early)
        loop(outer, to_far, outer - early + 1)
    else:
        loop(outer, to_far, 1)
    wait_map(3)
    total = adapter_delta(1)
    total = total + own_sum(0)
    for k in range(1, outer):
        s = (o + k) % outer
        remote(far_send.at[k], far_recv.at[s], far_send_sem.at[k], far_recv_sem.at[s], {"tensor": at(k, 0)}).wait_recv()
        total = total + far_recv[s].astype(F32)
    out[...] = total.astype(BF16)

    for copy in h_sends + map_copies + low_copies:
        copy.wait_send()
    for k in range(outer):
        if k > 0:
            far_copy(k).wait_send()
        if inner == 2:
            pair_copy(k).wait_send()
            if k > 0:
                forward(k).wait_send()


def per_device(tensor, replicas, *args):
    (
        hidden,
        w_query,
        output_weight,
        keys,
        values,
        query_down,
        query_up,
        output_down,
        output_up,
        adapter_ids,
        owner_map,
        kv_lengths,
    ) = args
    rows, width = hidden.shape
    cols = w_query.shape[1]
    stored, rank, _ = query_down.shape
    length, head_size = keys.shape[2:]
    kv_count = max(1, cols // head_size // (HEADS // KVS))
    inner = 2 if tensor % 2 == 0 else 1
    outer = tensor // inner
    lanes = max(128, rank)
    dma = pltpu.SemaphoreType.DMA
    any_spec = pl.BlockSpec(memory_space=pl.ANY)
    vmem_spec = pl.BlockSpec(memory_space=pltpu.VMEM)
    return pl.pallas_call(
        functools.partial(block_kernel, tensor, replicas),
        out_shape=pltpu.VMEM((rows, width), BF16),
        in_specs=[any_spec] * 9 + [vmem_spec] * 3,
        out_specs=vmem_spec,
        scratch_shapes=[
            pltpu.VMEM((tensor, rows, width), BF16),
            pltpu.VMEM((tensor, width, cols), BF16),
            pltpu.VMEM((tensor, cols, width), BF16),
            pltpu.VMEM((kv_count, rows, length, head_size), BF16),
            pltpu.VMEM((kv_count, rows, length, head_size), BF16),
            pltpu.VMEM((4, replicas * stored, rank, width), BF16),
            pltpu.VMEM((rows, cols), F32),
            pltpu.VMEM((rows, cols), F32),
            pltpu.VMEM((2, rows * rank // lanes, lanes), F32),
            pltpu.VMEM((2, tensor, rows * rank // lanes, lanes), F32),
            pltpu.VMEM((outer, rows, width), BF16),
            pltpu.VMEM((outer, rows, width), BF16),
            pltpu.VMEM((outer, rows, width), BF16),
            pltpu.VMEM((outer, rows, width), BF16),
            dma,
            dma((tensor,)),
            dma((tensor,)),
            dma((2, kv_count)),
            dma((4,)),
            dma((4, replicas)),
            dma((4, replicas)),
            dma((outer,)),
            dma((tensor,)),
            dma((outer,)),
            dma((2, tensor)),
            dma((2, tensor)),
            dma((outer,)),
            dma((outer,)),
            dma((outer,)),
            dma((outer,)),
        ],
        compiler_params=pltpu.CompilerParams(
            collective_id=0, has_side_effects=True, vmem_limit_bytes=58 * 1024 * 1024
        ),
    )(
        hidden,
        w_query,
        output_weight,
        keys,
        values,
        query_down,
        query_up,
        output_down,
        output_up,
        adapter_ids.reshape(1, -1),
        owner_map.reshape(1, -1),
        kv_lengths.reshape(1, -1),
    )


def solution(mesh):
    return jax.shard_map(
        functools.partial(per_device, mesh.shape["tensor"], mesh.shape["replica"]),
        mesh=mesh,
        in_specs=(
            P(("groups", "replica"), "tensor"),
            P(None, "tensor"),
            P("tensor", None),
            P(("groups", "replica"), None, None, None),
            P(("groups", "replica"), None, None, None),
            P(("groups", "replica"), None, "tensor"),
            P(("groups", "replica"), None, "tensor"),
            P(("groups", "replica"), None, "tensor"),
            P(("groups", "replica"), None, "tensor"),
            P("groups"),
            P("groups"),
            P(("groups", "replica")),
        ),
        out_specs=P(("groups", "replica"), "tensor"),
        check_vma=False,
    )
```

```python
import functools
import math

import jax
import jax.numpy as jnp
from jax import lax
from jax.experimental import pallas as pl
from jax.experimental.pallas import tpu as pltpu
from jax.sharding import PartitionSpec as P

HEADS = 64
KVS = 8
ROW_BLOCK = 8
F32 = jnp.float32
BF16 = jnp.bfloat16


def loop(count, body, first=0):
    def step(k, carry):
        body(k)
        return carry

    if count > first:
        lax.fori_loop(first, count, step, 0)


def remote(src, dst, send_sem, recv_sem, device):
    return pltpu.make_async_remote_copy(
        src_ref=src,
        dst_ref=dst,
        send_sem=send_sem,
        recv_sem=recv_sem,
        device_id=device,
        device_id_type=pl.DeviceIdType.MESH,
    )


def block_kernel(
    tensor,
    replicas,
    hidden,
    w_query,
    output_weight,
    keys,
    values,
    query_down,
    query_up,
    output_down,
    output_up,
    ids,
    owners,
    lengths,
    out,
    h_buf,
    wq_buf,
    ow_buf,
    key_buf,
    value_buf,
    map_buf,
    acc,
    mixed,
    low_send,
    low_recv,
    pair_send,
    pair_recv,
    far_send,
    far_recv,
    h_local,
    wq_sem,
    ow_sem,
    kv_sem,
    map_local,
    map_send_sem,
    map_recv_sem,
    h_send_sem,
    h_recv_sem,
    fwd_send_sem,
    low_send_sem,
    low_recv_sem,
    pair_send_sem,
    pair_recv_sem,
    far_send_sem,
    far_recv_sem,
):
    rows, width = hidden.shape
    cols = w_query.shape[1]
    head_size = keys.shape[3]
    length = keys.shape[2]
    stored, rank, _ = query_down.shape
    adapters = stored * replicas
    lanes = low_send.shape[2]
    packed = lanes // rank
    inner = 2 if tensor % 2 == 0 else 1
    outer = tensor // inner
    me = lax.axis_index("tensor")
    rep = lax.axis_index("replica")
    o, i = me // inner, me % inner

    def at(k, j):
        return ((o + k) % outer) * inner + (i + j) % inner

    barrier = pltpu.get_barrier_semaphore()
    for k in range(1, tensor):
        pl.semaphore_signal(
            barrier, inc=1, device_id={"tensor": (me + k) % tensor}, device_id_type=pl.DeviceIdType.MESH
        )
    for k in range(1, replicas):
        pl.semaphore_signal(
            barrier, inc=1, device_id={"replica": (rep + k) % replicas}, device_id_type=pl.DeviceIdType.MESH
        )

    own_hidden = pltpu.make_async_copy(hidden, h_buf.at[me], h_local)
    own_hidden.start()
    maps = (query_down, query_up, output_down, output_up)
    own_slots = pl.ds(pl.multiple_of(rep * stored, stored), stored)
    own_maps = [
        pltpu.make_async_copy(maps[m], map_buf.at[m, own_slots], map_local.at[m]) for m in range(4)
    ]

    def shard(n):
        return ((o + outer - n % outer) % outer) * inner + (i + n // outer) % inner

    def target(n):
        return at((n + 1) % outer, inner - 1 - n // outer)

    def wq_copy(s):
        return pltpu.make_async_copy(
            w_query.at[pl.ds(pl.multiple_of(s * width, width), width), :], wq_buf.at[s], wq_sem.at[s]
        )

    def ow_copy(s):
        return pltpu.make_async_copy(
            output_weight.at[:, pl.ds(pl.multiple_of(s * width, width), width)], ow_buf.at[s], ow_sem.at[s]
        )

    own_maps[0].start()
    local_heads = cols // head_size
    group = HEADS // KVS
    kv_count = max(1, local_heads // group)
    first_kv = me * local_heads // group
    kv_copies = []
    for j in range(kv_count):
        kv_copies.append(pltpu.make_async_copy(keys.at[:, first_kv + j], key_buf.at[j], kv_sem.at[0, j]))
        kv_copies.append(pltpu.make_async_copy(values.at[:, first_kv + j], value_buf.at[j], kv_sem.at[1, j]))
    ahead = min(4, tensor)
    for n in range(ahead):
        wq_copy(shard(n)).start()

    pl.semaphore_wait(barrier, tensor - 1 + replicas - 1)
    own_hidden.wait()

    h_sends = []
    if inner == 2:
        h_sends.append(
            remote(h_buf.at[me], h_buf.at[me], h_send_sem.at[0], h_recv_sem.at[me], {"tensor": at(0, 1)})
        )
    for k in range(1, outer):
        h_sends.append(
            remote(
                h_buf.at[me], h_buf.at[me], h_send_sem.at[k], h_recv_sem.at[me], {"tensor": at(k, 0)}
            )
        )
    for copy in h_sends:
        copy.start()

    map_copies = []

    def send_map(m):
        for k in range(1, replicas):
            map_copies.append(
                remote(
                    maps[m],
                    map_buf.at[m, own_slots],
                    map_send_sem.at[m, k],
                    map_recv_sem.at[m, rep],
                    {"replica": (rep + k) % replicas},
                )
            )
            map_copies[-1].start()

    send_map(0)
    own_maps[1].start()
    for copy in kv_copies:
        copy.start()

    def wait_map(m):
        own_maps[m].wait()
        for k in range(1, replicas):
            other = (rep + k) % replicas
            block = map_buf.at[m, pl.ds(pl.multiple_of(other * stored, stored), stored)]
            remote(block, block, map_send_sem.at[m, k], map_recv_sem.at[m, other], {"replica": other}).wait_recv()

    def down_rows(line, first):
        size = line.shape[1]
        row = lax.broadcasted_iota(jnp.int32, (rows, size), 0) + first
        column = lax.broadcasted_iota(jnp.int32, (rows, size), 1)
        return jnp.sum(jnp.where(row == column, line.astype(F32), 0.0), axis=1, keepdims=True)

    own_ids = down_rows(ids[...], rep * rows)
    held = down_rows(lengths[...], 0)
    table = lax.broadcasted_iota(jnp.int32, (rows, owners.shape[1]), 1).astype(F32)
    slot = jnp.sum(jnp.where(own_ids == table, owners[...].astype(F32), 0.0), axis=1, keepdims=True)
    lane = lax.broadcasted_iota(jnp.int32, (rows, adapters * rank), 1) // rank
    pick = lane.astype(F32) == slot
    lower = lax.broadcasted_iota(jnp.int32, (rows // packed, lanes), 1) < rank

    def turned(x):
        return jnp.concatenate([x[:, rank:], x[:, :rank]], axis=1)

    def send_low(which, features):
        down = map_buf[2 * which].reshape(adapters * rank, width)
        part = lax.dot_general(features, down, (((1,), (1,)), ((), ())), preferred_element_type=F32)
        part = jnp.where(pick, part, 0.0)
        part = sum(part[:, c : c + lanes] for c in range(0, adapters * rank, lanes))
        if packed == 2:
            part = part + turned(part)
            part = jnp.where(lower, part[: rows // 2], part[rows // 2 :])
        low_send[which] = part
        copies = []
        for k in range(1, tensor):
            copies.append(
                remote(
                    low_send.at[which],
                    low_recv.at[which, me],
                    low_send_sem.at[which, k],
                    low_recv_sem.at[which, me],
                    {"tensor": (me + k) % tensor},
                )
            )
            copies[-1].start()
        return copies

    def adapter_delta(which):
        total = low_send[which]
        for k in range(1, tensor):
            s = (me + k) % tensor
            remote(
                low_send.at[which], low_recv.at[which, s], low_send_sem.at[which, k], low_recv_sem.at[which, s], {"tensor": s}
            ).wait_recv()
            total = total + low_recv[which, s]
        if packed == 2:
            other = turned(total)
            total = jnp.concatenate(
                [jnp.where(lower, total, other), jnp.where(lower, other, total)], axis=0
            )
        spread = jnp.concatenate([total] * (adapters * rank // lanes), axis=1)
        spread = jnp.where(pick, spread, 0.0).astype(BF16)
        up = map_buf[2 * which + 1].reshape(adapters * rank, width)
        return 0.5 * jnp.dot(spread, up, preferred_element_type=F32)

    def wait_hidden(s):
        remote(h_buf.at[s], h_buf.at[s], h_send_sem.at[0], h_recv_sem.at[s], {"tensor": at(0, 1)}).wait_recv()

    acc[...] = jnp.zeros_like(acc)

    def forward(n):
        s = shard(n)
        return remote(h_buf.at[s], h_buf.at[s], fwd_send_sem.at[n], h_recv_sem.at[s], {"tensor": at(0, 1)})

    def use_shard(n):
        following = shard(n + 1)

        @pl.when(n + 1 < outer)
        def _():
            wait_hidden(following)
            if inner == 2:
                forward(n + 1).start()

        @pl.when(n + ahead < tensor)
        def _():
            wq_copy(shard(n + ahead)).start()

        ow_copy(target(n)).start()
        s = shard(n)

        @pl.when(n >= outer)
        def _():
            wait_hidden(s)

        wq_copy(s).wait()
        acc[...] += jnp.dot(h_buf[s], wq_buf[s], preferred_element_type=F32)

    first, second = tensor * 3 // 8, tensor * 7 // 8
    loop(first, use_shard)
    send_map(1)
    wait_map(0)
    low_copies = send_low(0, h_buf[me])
    loop(second, use_shard, first)
    wait_map(1)
    acc[...] += adapter_delta(0)
    loop(tensor, use_shard, second)
    for m in range(2, 4):
        send_map(m)
        own_maps[m].start()
    query = acc[...]

    for copy in kv_copies:
        copy.wait()
    per_kv = local_heads // kv_count
    shape = (per_kv * ROW_BLOCK, ROW_BLOCK * length)
    row = lax.broadcasted_iota(jnp.int32, shape, 0) % ROW_BLOCK
    column = lax.broadcasted_iota(jnp.int32, shape, 1)
    position = (column - row * length).astype(F32)
    for j in range(kv_count):
        for b in range(0, rows, ROW_BLOCK):
            heads = [
                query[b : b + ROW_BLOCK, h * head_size : (h + 1) * head_size]
                for h in range(j * per_kv, (j + 1) * per_kv)
            ]
            q = jnp.concatenate(heads, axis=0).astype(BF16)
            key = key_buf[j, b : b + ROW_BLOCK].reshape(ROW_BLOCK * length, head_size)
            value = value_buf[j, b : b + ROW_BLOCK].reshape(ROW_BLOCK * length, head_size)
            live = jnp.concatenate([held[b : b + ROW_BLOCK]] * per_kv, axis=0)
            scores = lax.dot_general(q, key, (((1,), (1,)), ((), ())), preferred_element_type=F32)
            scores = scores * (1.0 / math.sqrt(head_size))
            scores = jnp.where((position >= 0) & (position < live), scores, -1e30)
            top = jnp.max(scores, axis=1, keepdims=True)
            weights = jnp.exp(scores - top)
            probs = (weights / jnp.sum(weights, axis=1, keepdims=True)).astype(BF16)
            result = jnp.dot(probs, value, preferred_element_type=F32)
            for n in range(per_kv):
                h = j * per_kv + n
                mixed[b : b + ROW_BLOCK, h * head_size : (h + 1) * head_size] = result[
                    n * ROW_BLOCK : (n + 1) * ROW_BLOCK
                ]

    features = mixed[...].astype(BF16)
    def pair_copy(k):
        d = (o + k) % outer
        return remote(
            pair_send.at[k], pair_recv.at[d], pair_send_sem.at[k], pair_recv_sem.at[d], {"tensor": at(0, 1)}
        )

    def far_copy(k):
        return remote(far_send.at[k], far_recv.at[o], far_send_sem.at[k], far_recv_sem.at[o], {"tensor": at(k, 0)})

    def product(s):
        ow_copy(s).wait()
        return jnp.dot(features, ow_buf[s], preferred_element_type=F32)

    def to_pair(n):
        k = (n + 1) % outer
        pair_send[k] = product(at(k, 1)).astype(BF16)
        pair_copy(k).start()

    def own_sum(k):
        total = product(at(k, 0))
        if inner == 2:
            pair_copy(k).wait_recv()
            total = total + pair_recv[(o + k) % outer].astype(F32)
        return total

    def to_far(k):
        far_send[k] = own_sum(k).astype(BF16)
        far_copy(k).start()

    early = min(2, outer) if inner == 2 else 0
    loop(early, to_pair)
    wait_map(2)
    low_copies += send_low(1, features)

    def both(n):
        to_far(n - early + 1)
        to_pair(n)

    if inner == 2:
        loop(outer, both, early)
        loop(outer, to_far, outer - early + 1)
    else:
        loop(outer, to_far, 1)
    wait_map(3)
    total = adapter_delta(1)
    total = total + own_sum(0)
    for k in range(1, outer):
        s = (o + k) % outer
        remote(far_send.at[k], far_recv.at[s], far_send_sem.at[k], far_recv_sem.at[s], {"tensor": at(k, 0)}).wait_recv()
        total = total + far_recv[s].astype(F32)
    out[...] = total.astype(BF16)

    for copy in h_sends + map_copies + low_copies:
        copy.wait_send()
    for k in range(outer):
        if k > 0:
            far_copy(k).wait_send()
        if inner == 2:
            pair_copy(k).wait_send()
            if k > 0:
                forward(k).wait_send()


def per_device(tensor, replicas, *args):
    (
        hidden,
        w_query,
        output_weight,
        keys,
        values,
        query_down,
        query_up,
        output_down,
        output_up,
        adapter_ids,
        owner_map,
        kv_lengths,
    ) = args
    rows, width = hidden.shape
    cols = w_query.shape[1]
    stored, rank, _ = query_down.shape
    length, head_size = keys.shape[2:]
    kv_count = max(1, cols // head_size // (HEADS // KVS))
    inner = 2 if tensor % 2 == 0 else 1
    outer = tensor // inner
    lanes = max(128, rank)
    dma = pltpu.SemaphoreType.DMA
    any_spec = pl.BlockSpec(memory_space=pl.ANY)
    vmem_spec = pl.BlockSpec(memory_space=pltpu.VMEM)
    return pl.pallas_call(
        functools.partial(block_kernel, tensor, replicas),
        out_shape=pltpu.VMEM((rows, width), BF16),
        in_specs=[any_spec] * 9 + [vmem_spec] * 3,
        out_specs=vmem_spec,
        scratch_shapes=[
            pltpu.VMEM((tensor, rows, width), BF16),
            pltpu.VMEM((tensor, width, cols), BF16),
            pltpu.VMEM((tensor, cols, width), BF16),
            pltpu.VMEM((kv_count, rows, length, head_size), BF16),
            pltpu.VMEM((kv_count, rows, length, head_size), BF16),
            pltpu.VMEM((4, replicas * stored, rank, width), BF16),
            pltpu.VMEM((rows, cols), F32),
            pltpu.VMEM((rows, cols), F32),
            pltpu.VMEM((2, rows * rank // lanes, lanes), F32),
            pltpu.VMEM((2, tensor, rows * rank // lanes, lanes), F32),
            pltpu.VMEM((outer, rows, width), BF16),
            pltpu.VMEM((outer, rows, width), BF16),
            pltpu.VMEM((outer, rows, width), BF16),
            pltpu.VMEM((outer, rows, width), BF16),
            dma,
            dma((tensor,)),
            dma((tensor,)),
            dma((2, kv_count)),
            dma((4,)),
            dma((4, replicas)),
            dma((4, replicas)),
            dma((outer,)),
            dma((tensor,)),
            dma((outer,)),
            dma((2, tensor)),
            dma((2, tensor)),
            dma((outer,)),
            dma((outer,)),
            dma((outer,)),
            dma((outer,)),
        ],
        compiler_params=pltpu.CompilerParams(
            collective_id=0, has_side_effects=True, vmem_limit_bytes=58 * 1024 * 1024
        ),
    )(
        hidden,
        w_query,
        output_weight,
        keys,
        values,
        query_down,
        query_up,
        output_down,
        output_up,
        adapter_ids.reshape(1, -1),
        owner_map.reshape(1, -1),
        kv_lengths.reshape(1, -1),
    )


def solution(mesh):
    return jax.shard_map(
        functools.partial(per_device, mesh.shape["tensor"], mesh.shape["replica"]),
        mesh=mesh,
        in_specs=(
            P(("groups", "replica"), "tensor"),
            P(None, "tensor"),
            P("tensor", None),
            P(("groups", "replica"), None, None, None),
            P(("groups", "replica"), None, None, None),
            P(("groups", "replica"), None, "tensor"),
            P(("groups", "replica"), None, "tensor"),
            P(("groups", "replica"), None, "tensor"),
            P(("groups", "replica"), None, "tensor"),
            P("groups"),
            P("groups"),
            P(("groups", "replica")),
        ),
        out_specs=P(("groups", "replica"), "tensor"),
        check_vma=False,
    )
```

```python
import functools
import math

import jax
import jax.numpy as jnp
from jax import lax
from jax.experimental import pallas as pl
from jax.experimental.pallas import tpu as pltpu
from jax.sharding import PartitionSpec as P

HEADS = 64
KVS = 8
ROW_BLOCK = 8
F32 = jnp.float32
BF16 = jnp.bfloat16


def loop(count, body, first=0):
    def step(k, carry):
        body(k)
        return carry

    if count > first:
        lax.fori_loop(first, count, step, 0)


def remote(src, dst, send_sem, recv_sem, device):
    return pltpu.make_async_remote_copy(
        src_ref=src,
        dst_ref=dst,
        send_sem=send_sem,
        recv_sem=recv_sem,
        device_id=device,
        device_id_type=pl.DeviceIdType.MESH,
    )


def block_kernel(
    tensor,
    replicas,
    hidden,
    w_query,
    output_weight,
    keys,
    values,
    query_down,
    query_up,
    output_down,
    output_up,
    ids,
    owners,
    lengths,
    out,
    h_buf,
    wq_buf,
    ow_buf,
    key_buf,
    value_buf,
    map_buf,
    acc,
    mixed,
    low_send,
    low_recv,
    pair_send,
    pair_recv,
    far_send,
    far_recv,
    h_local,
    wq_sem,
    ow_sem,
    kv_sem,
    map_local,
    map_send_sem,
    map_recv_sem,
    h_send_sem,
    h_recv_sem,
    fwd_send_sem,
    low_send_sem,
    low_recv_sem,
    pair_send_sem,
    pair_recv_sem,
    far_send_sem,
    far_recv_sem,
):
    rows, width = hidden.shape
    cols = w_query.shape[1]
    head_size = keys.shape[3]
    length = keys.shape[2]
    stored, rank, _ = query_down.shape
    adapters = stored * replicas
    lanes = low_send.shape[2]
    packed = lanes // rank
    inner = 2 if tensor % 2 == 0 else 1
    outer = tensor // inner
    me = lax.axis_index("tensor")
    rep = lax.axis_index("replica")
    o, i = me // inner, me % inner

    def at(k, j):
        return ((o + k) % outer) * inner + (i + j) % inner

    barrier = pltpu.get_barrier_semaphore()
    for k in range(1, tensor):
        pl.semaphore_signal(
            barrier, inc=1, device_id={"tensor": (me + k) % tensor}, device_id_type=pl.DeviceIdType.MESH
        )
    for k in range(1, replicas):
        pl.semaphore_signal(
            barrier, inc=1, device_id={"replica": (rep + k) % replicas}, device_id_type=pl.DeviceIdType.MESH
        )

    own_hidden = pltpu.make_async_copy(hidden, h_buf.at[me], h_local)
    own_hidden.start()
    maps = (query_down, query_up, output_down, output_up)
    own_slots = pl.ds(pl.multiple_of(rep * stored, stored), stored)
    own_maps = [
        pltpu.make_async_copy(maps[m], map_buf.at[m, own_slots], map_local.at[m]) for m in range(4)
    ]

    def shard(n):
        return ((o + outer - n % outer) % outer) * inner + (i + n // outer) % inner

    def target(n):
        return at((n + 1) % outer, inner - 1 - n // outer)

    def wq_copy(s):
        return pltpu.make_async_copy(
            w_query.at[pl.ds(pl.multiple_of(s * width, width), width), :], wq_buf.at[s], wq_sem.at[s]
        )

    def ow_copy(s):
        return pltpu.make_async_copy(
            output_weight.at[:, pl.ds(pl.multiple_of(s * width, width), width)], ow_buf.at[s], ow_sem.at[s]
        )

    own_maps[0].start()
    local_heads = cols // head_size
    group = HEADS // KVS
    kv_count = max(1, local_heads // group)
    first_kv = me * local_heads // group
    kv_copies = []
    for j in range(kv_count):
        kv_copies.append(pltpu.make_async_copy(keys.at[:, first_kv + j], key_buf.at[j], kv_sem.at[0, j]))
        kv_copies.append(pltpu.make_async_copy(values.at[:, first_kv + j], value_buf.at[j], kv_sem.at[1, j]))
    ahead = min(4, tensor)
    for n in range(ahead):
        wq_copy(shard(n)).start()

    pl.semaphore_wait(barrier, tensor - 1 + replicas - 1)
    own_hidden.wait()

    h_sends = []
    if inner == 2:
        h_sends.append(
            remote(h_buf.at[me], h_buf.at[me], h_send_sem.at[0], h_recv_sem.at[me], {"tensor": at(0, 1)})
        )
    for k in range(1, outer):
        h_sends.append(
            remote(
                h_buf.at[me], h_buf.at[me], h_send_sem.at[k], h_recv_sem.at[me], {"tensor": at(k, 0)}
            )
        )
    for copy in h_sends:
        copy.start()

    map_copies = []

    def send_map(m):
        for k in range(1, replicas):
            map_copies.append(
                remote(
                    maps[m],
                    map_buf.at[m, own_slots],
                    map_send_sem.at[m, k],
                    map_recv_sem.at[m, rep],
                    {"replica": (rep + k) % replicas},
                )
            )
            map_copies[-1].start()

    send_map(0)
    own_maps[1].start()
    for copy in kv_copies:
        copy.start()

    def wait_map(m):
        own_maps[m].wait()
        for k in range(1, replicas):
            other = (rep + k) % replicas
            block = map_buf.at[m, pl.ds(pl.multiple_of(other * stored, stored), stored)]
            remote(block, block, map_send_sem.at[m, k], map_recv_sem.at[m, other], {"replica": other}).wait_recv()

    def down_rows(line, first):
        size = line.shape[1]
        row = lax.broadcasted_iota(jnp.int32, (rows, size), 0) + first
        column = lax.broadcasted_iota(jnp.int32, (rows, size), 1)
        return jnp.sum(jnp.where(row == column, line.astype(F32), 0.0), axis=1, keepdims=True)

    own_ids = down_rows(ids[...], rep * rows)
    held = down_rows(lengths[...], 0)
    table = lax.broadcasted_iota(jnp.int32, (rows, owners.shape[1]), 1).astype(F32)
    slot = jnp.sum(jnp.where(own_ids == table, owners[...].astype(F32), 0.0), axis=1, keepdims=True)
    lane = lax.broadcasted_iota(jnp.int32, (rows, adapters * rank), 1) // rank
    pick = lane.astype(F32) == slot
    lower = lax.broadcasted_iota(jnp.int32, (rows // packed, lanes), 1) < rank

    def turned(x):
        return jnp.concatenate([x[:, rank:], x[:, :rank]], axis=1)

    def send_low(which, features):
        down = map_buf[2 * which].reshape(adapters * rank, width)
        part = lax.dot_general(features, down, (((1,), (1,)), ((), ())), preferred_element_type=F32)
        part = jnp.where(pick, part, 0.0)
        part = sum(part[:, c : c + lanes] for c in range(0, adapters * rank, lanes))
        if packed == 2:
            part = part + turned(part)
            part = jnp.where(lower, part[: rows // 2], part[rows // 2 :])
        low_send[which] = part
        copies = []
        for k in range(1, tensor):
            copies.append(
                remote(
                    low_send.at[which],
                    low_recv.at[which, me],
                    low_send_sem.at[which, k],
                    low_recv_sem.at[which, me],
                    {"tensor": (me + k) % tensor},
                )
            )
            copies[-1].start()
        return copies

    def adapter_delta(which):
        total = low_send[which]
        for k in range(1, tensor):
            s = (me + k) % tensor
            remote(
                low_send.at[which], low_recv.at[which, s], low_send_sem.at[which, k], low_recv_sem.at[which, s], {"tensor": s}
            ).wait_recv()
            total = total + low_recv[which, s]
        if packed == 2:
            other = turned(total)
            total = jnp.concatenate(
                [jnp.where(lower, total, other), jnp.where(lower, other, total)], axis=0
            )
        spread = jnp.concatenate([total] * (adapters * rank // lanes), axis=1)
        spread = jnp.where(pick, spread, 0.0).astype(BF16)
        up = map_buf[2 * which + 1].reshape(adapters * rank, width)
        return 0.5 * jnp.dot(spread, up, preferred_element_type=F32)

    def wait_hidden(s):
        remote(h_buf.at[s], h_buf.at[s], h_send_sem.at[0], h_recv_sem.at[s], {"tensor": at(0, 1)}).wait_recv()

    acc[...] = jnp.zeros_like(acc)

    def forward(n):
        s = shard(n)
        return remote(h_buf.at[s], h_buf.at[s], fwd_send_sem.at[n], h_recv_sem.at[s], {"tensor": at(0, 1)})

    def use_shard(n):
        following = shard(n + 1)

        @pl.when(n + 1 < outer)
        def _():
            wait_hidden(following)
            if inner == 2:
                forward(n + 1).start()

        @pl.when(n + ahead < tensor)
        def _():
            wq_copy(shard(n + ahead)).start()

        ow_copy(target(n)).start()
        s = shard(n)

        @pl.when(n >= outer)
        def _():
            wait_hidden(s)

        wq_copy(s).wait()
        acc[...] += jnp.dot(h_buf[s], wq_buf[s], preferred_element_type=F32)

    first, second = tensor * 3 // 8, tensor * 7 // 8
    loop(first, use_shard)
    send_map(1)
    wait_map(0)
    low_copies = send_low(0, h_buf[me])
    send_map(2)
    own_maps[2].start()
    loop(second, use_shard, first)
    wait_map(1)
    acc[...] += adapter_delta(0)
    loop(tensor, use_shard, second)
    send_map(3)
    own_maps[3].start()
    query = acc[...]

    for copy in kv_copies:
        copy.wait()
    per_kv = local_heads // kv_count
    shape = (per_kv * ROW_BLOCK, ROW_BLOCK * length)
    row = lax.broadcasted_iota(jnp.int32, shape, 0) % ROW_BLOCK
    column = lax.broadcasted_iota(jnp.int32, shape, 1)
    position = (column - row * length).astype(F32)
    for j in range(kv_count):
        for b in range(0, rows, ROW_BLOCK):
            heads = [
                query[b : b + ROW_BLOCK, h * head_size : (h + 1) * head_size]
                for h in range(j * per_kv, (j + 1) * per_kv)
            ]
            q = jnp.concatenate(heads, axis=0).astype(BF16)
            key = key_buf[j, b : b + ROW_BLOCK].reshape(ROW_BLOCK * length, head_size)
            value = value_buf[j, b : b + ROW_BLOCK].reshape(ROW_BLOCK * length, head_size)
            live = jnp.concatenate([held[b : b + ROW_BLOCK]] * per_kv, axis=0)
            scores = lax.dot_general(q, key, (((1,), (1,)), ((), ())), preferred_element_type=F32)
            scores = scores * (1.0 / math.sqrt(head_size))
            scores = jnp.where((position >= 0) & (position < live), scores, -1e30)
            top = jnp.max(scores, axis=1, keepdims=True)
            weights = jnp.exp(scores - top)
            probs = (weights / jnp.sum(weights, axis=1, keepdims=True)).astype(BF16)
            result = jnp.dot(probs, value, preferred_element_type=F32)
            for n in range(per_kv):
                h = j * per_kv + n
                mixed[b : b + ROW_BLOCK, h * head_size : (h + 1) * head_size] = result[
                    n * ROW_BLOCK : (n + 1) * ROW_BLOCK
                ]

    features = mixed[...].astype(BF16)
    def pair_copy(k):
        d = (o + k) % outer
        return remote(
            pair_send.at[k], pair_recv.at[d], pair_send_sem.at[k], pair_recv_sem.at[d], {"tensor": at(0, 1)}
        )

    def far_copy(k):
        return remote(far_send.at[k], far_recv.at[o], far_send_sem.at[k], far_recv_sem.at[o], {"tensor": at(k, 0)})

    def product(s):
        ow_copy(s).wait()
        return jnp.dot(features, ow_buf[s], preferred_element_type=F32)

    def to_pair(n):
        k = (n + 1) % outer
        pair_send[k] = product(at(k, 1)).astype(BF16)
        pair_copy(k).start()

    def own_sum(k):
        total = product(at(k, 0))
        if inner == 2:
            pair_copy(k).wait_recv()
            total = total + pair_recv[(o + k) % outer].astype(F32)
        return total

    def to_far(k):
        far_send[k] = own_sum(k).astype(BF16)
        far_copy(k).start()

    early = min(2, outer) if inner == 2 else 0
    loop(early, to_pair)
    wait_map(2)
    low_copies += send_low(1, features)

    def both(n):
        to_far(n - early + 1)
        to_pair(n)

    if inner == 2:
        loop(outer, both, early)
        loop(outer, to_far, outer - early + 1)
    else:
        loop(outer, to_far, 1)
    wait_map(3)
    total = adapter_delta(1)
    total = total + own_sum(0)
    for k in range(1, outer):
        s = (o + k) % outer
        remote(far_send.at[k], far_recv.at[s], far_send_sem.at[k], far_recv_sem.at[s], {"tensor": at(k, 0)}).wait_recv()
        total = total + far_recv[s].astype(F32)
    out[...] = total.astype(BF16)

    for copy in h_sends + map_copies + low_copies:
        copy.wait_send()
    for k in range(outer):
        if k > 0:
            far_copy(k).wait_send()
        if inner == 2:
            pair_copy(k).wait_send()
            if k > 0:
                forward(k).wait_send()


def per_device(tensor, replicas, *args):
    (
        hidden,
        w_query,
        output_weight,
        keys,
        values,
        query_down,
        query_up,
        output_down,
        output_up,
        adapter_ids,
        owner_map,
        kv_lengths,
    ) = args
    rows, width = hidden.shape
    cols = w_query.shape[1]
    stored, rank, _ = query_down.shape
    length, head_size = keys.shape[2:]
    kv_count = max(1, cols // head_size // (HEADS // KVS))
    inner = 2 if tensor % 2 == 0 else 1
    outer = tensor // inner
    lanes = max(128, rank)
    dma = pltpu.SemaphoreType.DMA
    any_spec = pl.BlockSpec(memory_space=pl.ANY)
    vmem_spec = pl.BlockSpec(memory_space=pltpu.VMEM)
    return pl.pallas_call(
        functools.partial(block_kernel, tensor, replicas),
        out_shape=pltpu.VMEM((rows, width), BF16),
        in_specs=[any_spec] * 9 + [vmem_spec] * 3,
        out_specs=vmem_spec,
        scratch_shapes=[
            pltpu.VMEM((tensor, rows, width), BF16),
            pltpu.VMEM((tensor, width, cols), BF16),
            pltpu.VMEM((tensor, cols, width), BF16),
            pltpu.VMEM((kv_count, rows, length, head_size), BF16),
            pltpu.VMEM((kv_count, rows, length, head_size), BF16),
            pltpu.VMEM((4, replicas * stored, rank, width), BF16),
            pltpu.VMEM((rows, cols), F32),
            pltpu.VMEM((rows, cols), F32),
            pltpu.VMEM((2, rows * rank // lanes, lanes), F32),
            pltpu.VMEM((2, tensor, rows * rank // lanes, lanes), F32),
            pltpu.VMEM((outer, rows, width), BF16),
            pltpu.VMEM((outer, rows, width), BF16),
            pltpu.VMEM((outer, rows, width), BF16),
            pltpu.VMEM((outer, rows, width), BF16),
            dma,
            dma((tensor,)),
            dma((tensor,)),
            dma((2, kv_count)),
            dma((4,)),
            dma((4, replicas)),
            dma((4, replicas)),
            dma((outer,)),
            dma((tensor,)),
            dma((outer,)),
            dma((2, tensor)),
            dma((2, tensor)),
            dma((outer,)),
            dma((outer,)),
            dma((outer,)),
            dma((outer,)),
        ],
        compiler_params=pltpu.CompilerParams(
            collective_id=0, has_side_effects=True, vmem_limit_bytes=58 * 1024 * 1024
        ),
    )(
        hidden,
        w_query,
        output_weight,
        keys,
        values,
        query_down,
        query_up,
        output_down,
        output_up,
        adapter_ids.reshape(1, -1),
        owner_map.reshape(1, -1),
        kv_lengths.reshape(1, -1),
    )


def solution(mesh):
    return jax.shard_map(
        functools.partial(per_device, mesh.shape["tensor"], mesh.shape["replica"]),
        mesh=mesh,
        in_specs=(
            P(("groups", "replica"), "tensor"),
            P(None, "tensor"),
            P("tensor", None),
            P(("groups", "replica"), None, None, None),
            P(("groups", "replica"), None, None, None),
            P(("groups", "replica"), None, "tensor"),
            P(("groups", "replica"), None, "tensor"),
            P(("groups", "replica"), None, "tensor"),
            P(("groups", "replica"), None, "tensor"),
            P("groups"),
            P("groups"),
            P(("groups", "replica")),
        ),
        out_specs=P(("groups", "replica"), "tensor"),
        check_vma=False,
    )
```
